256 devices in a mesh: dp: 32 (over x, z_hi, core), tensor: 8 (over z_lo, y).
Axes of the slice: x: 4, y: 4, z: 8 (z_hi: 4, z_lo: 2; z = z_hi * 2 + z_lo), core: 2. Of those that a mesh axis runs over, the one named last changes fastest.
Arguments:
- acts: bfloat16 [8192, 4096], P('dp', 'tensor'), may hold values from -6 to 6
- cotangent: bfloat16 [8192, 5120], P('dp', 'tensor'), may hold values from -6 to 6
- out_weight: bfloat16 [4096, 5120], P('tensor'), may hold values from -0.09375 to 0.09375
- old_a: bfloat16 [32, 128, 64], P('tensor'), may hold values from -0.09375 to 0.09375
- old_b: bfloat16 [64, 5120], replicated, may hold values from -0.75 to 0.75
- master_a: float32 [32, 128, 64], P('tensor', 'dp'), may hold values from -0.09375 to 0.09375
- master_b: float32 [64, 5120], P('dp', 'tensor'), may hold values from -0.75 to 0.75
- moment_a: float32 [32, 128, 64], P('tensor', 'dp'), may hold values from -0.15625 to 0.15625
- moment_b: float32 [64, 5120], P('dp', 'tensor'), may hold values from -0.15625 to 0.15625
- second_a: float32 [32, 128, 64], P('tensor', 'dp'), may hold values from 0.0001 to 0.01
- second_b: float32 [64, 5120], P('dp', 'tensor'), may hold values from 0.0001 to 0.01
- key_cache: bfloat16 [4096, 8, 48, 128], P('dp', 'tensor'), may hold values from -6 to 6
- value_cache: bfloat16 [4096, 8, 48, 128], P('dp', 'tensor'), may hold values from -6 to 6
- lengths: int32 [4096], P('dp'), may hold values from 1 to 48, as said below
- new_query: bfloat16 [4096, 3, 4096], P('dp', None, 'tensor'), may hold values from -100 to 100
- new_key: bfloat16 [4096, 3, 1024], P('dp', None, 'tensor'), may hold values from -8 to 8
- new_value: bfloat16 [4096, 3, 1024], P('dp', None, 'tensor'), may hold values from -6 to 6
Outputs:
- attention_output_gradient: bfloat16 [8192, 4096], P('dp', 'tensor')
- new_master_a: float32 [32, 128, 64], P('tensor', 'dp')
- new_master_b: float32 [64, 5120], P('dp', 'tensor')
- new_moment_a: float32 [32, 128, 64], P('tensor', 'dp')
- new_moment_b: float32 [64, 5120], P('dp', 'tensor')
- new_second_a: float32 [32, 128, 64], P('tensor', 'dp')
- new_second_b: float32 [64, 5120], P('dp', 'tensor')
- decoded_projection_output: bfloat16 [5120, 12288], P('tensor', 'dp')
The draws below stay inside these ranges and needn't reach their ends.
Inputs may be any that keep to these rules, and one draw needn't show every extreme that they name: `lengths`: every rollout group has a row that fills all 48 slots.
All inputs are finite; a program needn't handle non-finite values.
Results may differ from the reference program's by a relative error of at most 0.0067.
Values may be sent and summed in bfloat16 or wider, within the bound.
A program may use at most 128 MiB of HBM per device.

```python
import math
import jax
import jax.numpy as jnp
from jax import lax

D = 5120
HQ = 32
KVH = 8
HD = 128
RANK = 64
NEW = 3
ROWS = 128
CACHE = 48
TRAIN_TOKEN_TOTAL = 8192
BATCH = 4096
N_DP = 32


def shared_keys(key):
    return jax.random.normal(jax.random.fold_in(key, 11), (BATCH, NEW, KVH * HD), jnp.float32)


def draw_lengths(key, part):
    key = jax.random.fold_in(key, 3)
    drawn = jax.random.randint(key, (BATCH,), 1, CACHE + 1)
    first = jnp.arange(BATCH) % ROWS == 0
    return jnp.where(first, CACHE, drawn).astype(jnp.int32)


def draw_new_key(key, part):
    frozen_projection = shared_keys(key)
    return jnp.clip(frozen_projection, -8.0, 8.0).astype(jnp.bfloat16)


def draw_new_query(key, part):
    key = jax.random.fold_in(key, 7)
    entries = jax.random.normal(key, (BATCH, NEW, HQ * HD), jnp.float32)
    return jnp.clip(entries, -100.0, 100.0).astype(jnp.bfloat16)


def levels(stream_key, shape, split, least, top_value):
    loudness, own = 1.0, jax.random.fold_in(stream_key, 6)
    for axis_at, shards_of in split:
        steps = jnp.exp(jax.random.uniform(jax.random.fold_in(own, axis_at), (shards_of,), jnp.float32, least / len(split), top_value / len(split)))
        loudness = loudness * jnp.repeat(steps, shape[axis_at] // shards_of).reshape([-1 if axis == axis_at else 1 for axis in range(len(shape))])
    return loudness


def centred(stream_key, shape, width, most, shards=(), kind=jnp.bfloat16):
    level = levels(stream_key, shape, shards, -0.22, 0.18) if shards else 1.0
    values = jax.random.normal(stream_key, shape, jnp.float32) * width * level
    return jnp.minimum(jnp.maximum(values, -most), most).astype(kind)


def setup_inputs(seed: int = 0) -> dict:
    key_of = jax.random.split(jax.random.key(seed), 18)
    return {
        "acts": centred(key_of[0], (TRAIN_TOKEN_TOTAL, HQ * HD), 1.0, 6.0, ((0, 32), (1, 8))),
        "cotangent": centred(key_of[1], (TRAIN_TOKEN_TOTAL, D), 1.0, 6.0, ((0, 32), (1, 8))),
        "out_weight": centred(key_of[2], (HQ * HD, D), (HQ * HD) ** -0.5, 0.09375, ((0, 8),)),
        "old_a": centred(key_of[3], (HQ, HD, RANK), (HQ * HD) ** -0.5, 0.09375, ((0, 8),)),
        "old_b": centred(key_of[4], (RANK, D), RANK ** -0.5, 0.75),
        "master_a": centred(key_of[5], (HQ, HD, RANK), (HQ * HD) ** -0.5, 0.09375, ((0, 8), (1, 32)), jnp.float32),
        "master_b": centred(key_of[6], (RANK, D), RANK ** -0.5, 0.75, ((0, 32), (1, 8)), jnp.float32),
        "moment_a": centred(key_of[7], (HQ, HD, RANK), 0.01, 0.15625, ((0, 8), (1, 32)), jnp.float32),
        "moment_b": centred(key_of[8], (RANK, D), 0.01, 0.15625, ((0, 32), (1, 8)), jnp.float32),
        "second_a": jnp.clip(jnp.exp(math.log(0.01) - 4.6051702 * jax.random.uniform(key_of[9], (HQ, HD, RANK), jnp.float32) ** levels(key_of[9], (HQ, HD, RANK), ((0, 8), (1, 32)), -0.2, 0.2)), 0.0001, 0.01),
        "second_b": jnp.clip(jnp.exp(math.log(0.01) - 4.6051702 * jax.random.uniform(key_of[10], (RANK, D), jnp.float32) ** levels(key_of[10], (RANK, D), ((0, 32), (1, 8)), -0.2, 0.2)), 0.0001, 0.01),
        "key_cache": centred(key_of[11], (BATCH, KVH, CACHE, HD), 1.0, 6.0, ((0, 32), (1, 8))),
        "value_cache": centred(key_of[12], (BATCH, KVH, CACHE, HD), 1.0, 6.0, ((0, 32), (1, 8))),
        "lengths": draw_lengths(jax.random.fold_in(key_of[17], 71), 0),
        "new_query": draw_new_query(jax.random.fold_in(key_of[17], 71), 0),
        "new_key": draw_new_key(jax.random.fold_in(key_of[17], 71), 0),
        "new_value": centred(key_of[16], (BATCH, NEW, KVH * HD), 1.0, 6.0, ((0, 32), (2, 8))),
    }


adapter_scale = 2.0
beta_one = 0.9
beta_two = 0.999
learn_rate = 0.01
decay_rate = 0.01
corr_one = 1.0 - 0.9 ** 10
corr_two = 1.0 - 0.999 ** 10

def adam_step(master, moment, second, grad):
    moment_new = beta_one * moment + (1.0 - beta_one) * grad
    second_new = beta_two * second + (1.0 - beta_two) * grad * grad
    update = moment_new / corr_one / (jnp.sqrt(second_new / corr_two) + 1e-08)
    return (master - learn_rate * (update + decay_rate * master), moment_new, second_new)

def attend_block(query, keys, values, lengths, new_key, new_value):
    rows = query.shape[0]
    steps = query.shape[1]
    kv_heads = keys.shape[1]
    head_size = keys.shape[3]
    slots = keys.shape[2]
    group = query.shape[2] // (kv_heads * head_size)
    qf = query.astype(jnp.float32).reshape(rows, steps, kv_heads, group, head_size)
    knew = new_key.astype(jnp.float32).reshape(rows, steps, kv_heads, head_size)
    vnew = new_value.astype(jnp.float32).reshape(rows, steps, kv_heads, head_size)
    adapter_factor = 1.0 / jnp.sqrt(jnp.float32(head_size))
    cache_scores = jnp.einsum('bsngd,bncd->bsngc', qf, keys.astype(jnp.float32)) * adapter_factor
    fresh_scores = jnp.einsum('bsngd,btnd->bsngt', qf, knew) * adapter_factor
    cache_mask = (jnp.arange(slots)[None, :] < lengths[:, None])[:, None, None, None, :]
    fresh_mask = (jnp.arange(steps)[None, :] <= jnp.arange(steps)[:, None])[None, :, None, None, :]
    cache_scores = jnp.where(cache_mask, cache_scores, -1e+30)
    fresh_scores = jnp.where(fresh_mask, fresh_scores, -1e+30)
    top = jnp.maximum(lax.optimization_barrier(jnp.max(cache_scores, axis=-1)), lax.optimization_barrier(jnp.max(fresh_scores, axis=-1)))
    cache_exp = jnp.exp(cache_scores - top[..., None])
    fresh_exp = jnp.exp(fresh_scores - top[..., None])
    total = lax.optimization_barrier(jnp.sum(cache_exp, axis=-1)) + lax.optimization_barrier(jnp.sum(fresh_exp, axis=-1))
    cache_prob = (cache_exp / total[..., None]).astype(jnp.bfloat16)
    fresh_prob = (fresh_exp / total[..., None]).astype(jnp.bfloat16)
    combined_output = jnp.einsum('bsngc,bncd->bsngd', cache_prob.astype(jnp.float32), values.astype(jnp.float32))
    combined_output = combined_output + jnp.einsum('bsngt,btnd->bsngd', fresh_prob.astype(jnp.float32), vnew)
    return combined_output.astype(jnp.bfloat16).reshape(rows * steps, kv_heads * group * head_size)

def reference(acts, cotangent, out_weight, old_a, old_b, master_a, master_b, moment_a, moment_b, second_a, second_b, key_cache, value_cache, lengths, new_query, new_key, new_value):
    previous_down_factor = old_a.reshape(HQ * HD, RANK)
    acts_low = jnp.dot(acts, previous_down_factor, preferred_element_type=jnp.float32).astype(jnp.bfloat16)
    passed_down = jnp.dot(cotangent, old_b.T, preferred_element_type=jnp.float32).astype(jnp.bfloat16)
    attention_output_gradient = jnp.dot(cotangent, out_weight.T, preferred_element_type=jnp.float32)
    attention_output_gradient = (attention_output_gradient + adapter_scale * jnp.dot(passed_down, previous_down_factor.T, preferred_element_type=jnp.float32)).astype(jnp.bfloat16)
    adapter_factor = adapter_scale / TRAIN_TOKEN_TOTAL
    grad_a = (adapter_factor * jnp.dot(acts.T, passed_down, preferred_element_type=jnp.float32)).reshape(HQ, HD, RANK)
    grad_b = adapter_factor * jnp.dot(acts_low.T, cotangent, preferred_element_type=jnp.float32)
    new_a, mom_a, sec_a = adam_step(master_a, moment_a, second_a, grad_a)
    new_b, mom_b, sec_b = adam_step(master_b, moment_b, second_b, grad_b)
    a_new = new_a.astype(jnp.bfloat16).reshape(HQ * HD, RANK)
    updated_up_factor = new_b.astype(jnp.bfloat16)

    def one_group(index):
        start = index * ROWS
        query = lax.dynamic_slice_in_dim(new_query, start, ROWS, 0)
        keys = lax.dynamic_slice_in_dim(key_cache, start, ROWS, 0)
        values = lax.dynamic_slice_in_dim(value_cache, start, ROWS, 0)
        lens = lax.dynamic_slice_in_dim(lengths, start, ROWS, 0)
        knew = lax.dynamic_slice_in_dim(new_key, start, ROWS, 0)
        vnew = lax.dynamic_slice_in_dim(new_value, start, ROWS, 0)
        return attend_block(query, keys, values, lens, knew, vnew)
    attended = lax.map(one_group, jnp.arange(N_DP, dtype=jnp.int32)).reshape(BATCH * NEW, HQ * HD)
    frozen_projection = jnp.dot(attended, out_weight, preferred_element_type=jnp.float32)
    reduced_rank_input = jnp.dot(attended, a_new, preferred_element_type=jnp.float32)
    adapter_branch = jnp.dot(reduced_rank_input, updated_up_factor.astype(jnp.float32), precision=lax.Precision.HIGHEST)
    decoded_projection_output = (frozen_projection + adapter_scale * adapter_branch).astype(jnp.bfloat16).T
    return (attention_output_gradient, new_a, new_b, mom_a, mom_b, sec_a, sec_b, decoded_projection_output)
```

```python
import functools

import jax
import jax.numpy as jnp
from jax import lax
from jax.experimental import pallas as pl
from jax.experimental.pallas import tpu as pltpu
from jax.sharding import PartitionSpec as P

adapter_scale = 2.0
beta_one = 0.9
beta_two = 0.999
learn_rate = 0.01
decay_rate = 0.01
corr_one = 1.0 - 0.9**10
corr_two = 1.0 - 0.999**10
MESH = pl.DeviceIdType.MESH
f32 = jnp.float32
bf16 = jnp.bfloat16
NT = (((1,), (1,)), ((), ()))
NN = (((1,), (0,)), ((), ()))


def mm(a, b, dims=NN):
    return lax.dot_general(a, b, dims, preferred_element_type=f32)


def iota(shape, dim):
    return lax.broadcasted_iota(jnp.int32, shape, dim)


def onehot(hit):
    return jnp.where(hit, 1.0, 0.0).astype(f32).astype(bf16)


def adam_step(master, moment, second, grad):
    moment_new = beta_one * moment + (1.0 - beta_one) * grad
    second_new = beta_two * second + (1.0 - beta_two) * grad * grad
    update = moment_new / corr_one / (jnp.sqrt(second_new / corr_two) + 1e-08)
    return (master - learn_rate * (update + decay_rate * master), moment_new, second_new)


def kernel(
    acts_h, cot_h, w_h, olda_h, oldb_h,
    ma, mb, oa, ob, va, vb,
    key_h, val_h, len_ref, q_h, nk_h, nv_h,
    grad_o, nma_o, nmb_o, noa_o, nob_o, nva_o, nvb_o, out_o,
    acts, cot, w, olda, oldb, keys, vals, q, nk, nv,
    perma, spread, gather, permr, slotm, freshb, lencol,
    part, prs, lows, lowf, cgat, gacc,
    gst, gpeer, hsum, hrecv, ga_s, gb_s, fac,
    att, attp, att2, ysend, yown, yrecv, lsend, lrecv,
    lsem, s_prs, r_prs, s_pag, r_pag, s_cot, r_cot, s_core, r_core, s_dp, r_dp,
    s_fac, r_fac, s_fcore, r_fcore, s_y, r_y, s_low, r_low,
):
    dp = lax.axis_index("dp")
    t = lax.axis_index("tensor")
    chip = dp // 2
    core = dp % 2

    def tpeer(k):
        return (dp, (t + k) % 8)

    def cpeer(k):
        return (((chip + k) % 16) * 2 + core, t)

    corepeer = (chip * 2 + 1 - core, t)

    def remote(src, dst, ssem, rsem, dev):
        return pltpu.make_async_remote_copy(
            src_ref=src, dst_ref=dst, send_sem=ssem, recv_sem=rsem, device_id=dev, device_id_type=MESH
        )

    def drain(ref, sem):
        pltpu.make_async_copy(ref, ref, sem).wait()

    loads = [
        pltpu.make_async_copy(acts_h, acts, lsem.at[0]),
        pltpu.make_async_copy(cot_h, cot, lsem.at[1]),
        pltpu.make_async_copy(olda_h, olda, lsem.at[2]),
        pltpu.make_async_copy(oldb_h.at[:, pl.ds(pl.multiple_of(t * 640, 128), 640)], oldb, lsem.at[3]),
        pltpu.make_async_copy(q_h, q, lsem.at[4]),
        pltpu.make_async_copy(key_h, keys, lsem.at[5]),
        pltpu.make_async_copy(nk_h, nk, lsem.at[6]),
        pltpu.make_async_copy(val_h, vals, lsem.at[7]),
        pltpu.make_async_copy(nv_h, nv, lsem.at[8]),
    ]
    for j in range(8):
        loads.append(pltpu.make_async_copy(w_h.at[:, pl.ds(j * 640, 640)], w.at[j], lsem.at[9 + j]))
    for c in loads:
        c.start()

    bar = pltpu.get_barrier_semaphore()

    def sig_t(k, _):
        pl.semaphore_signal(bar, inc=1, device_id=tpeer(k), device_id_type=MESH)
        return 0

    def sig_c(k, _):
        pl.semaphore_signal(bar, inc=1, device_id=cpeer(k), device_id_type=MESH)
        return 0

    lax.fori_loop(1, 8, sig_t, 0)
    lax.fori_loop(1, 16, sig_c, 0)
    pl.semaphore_signal(bar, inc=1, device_id=corepeer, device_id_type=MESH)

    for c in loads[:4]:
        c.wait()
    low_p = mm(acts[:, 0:128], olda[0], NT)
    for h in range(1, 4):
        low_p += mm(acts[:, h * 128 : (h + 1) * 128], olda[h], NT)
    thr_p = mm(cot[...], oldb[...], NT)
    part[...] = jnp.concatenate([low_p, thr_p], axis=1).reshape(8, 32, 128)
    pl.semaphore_wait(bar, 23)

    def send_part(k, _):
        remote(part.at[(t + k) % 8], prs.at[7 - k], s_prs, r_prs, tpeer(k)).start()
        return 0

    lax.fori_loop(1, 8, send_part, 0)

    def send_cot(k, _):
        remote(cot, cgat.at[7 - k], s_cot, r_cot.at[7 - k], tpeer(k)).start()
        return 0

    lax.fori_loop(1, 8, send_cot, 0)

    prow, pcol = iota((512, 512), 0), iota((512, 512), 1)
    blk = prow >> 4
    perma[...] = onehot(
        pcol == (((prow >> 2) & 3) << 7) + (((blk & 15) * 2 + (blk >> 4)) << 2) + (prow & 3)
    )
    erow, ecol = iota((512, 320), 0), iota((512, 320), 1)
    blk = erow >> 4
    idx = erow & 15
    spread[...] = onehot(
        (idx < 10) & (ecol == ((idx >> 1) << 6) + ((blk & 15) * 2 + (blk >> 4)) * 2 + (idx & 1))
    )
    erow, ecol = iota((320, 512), 1), iota((320, 512), 0)
    blk = erow >> 4
    idx = erow & 15
    gather[...] = onehot(
        (idx < 10) & (ecol == ((idx >> 1) << 6) + ((blk & 15) * 2 + (blk >> 4)) * 2 + (idx & 1))
    )
    rj, rk = iota((384, 384), 0), iota((384, 384), 1)
    permr[...] = onehot((rj - 3 * (rk & 127)) == (rk >> 7))
    slot = iota((16, 768), 1) - 48 * iota((16, 768), 0)
    slotm[...] = jnp.where((slot >= 0) & (slot < 48), slot, 1000)
    fr, fc = iota((192, 48), 0), iota((192, 48), 1)
    freshb[...] = jnp.where(((fr & 15) == (fc & 15)) & ((fc >> 4) <= (fr >> 6)), 0.0, -1e30).astype(f32)
    diag = iota((128, 128), 0) == iota((128, 128), 1)
    lencol[...] = jnp.broadcast_to(
        jnp.sum(jnp.where(diag, len_ref[...].astype(f32), 0.0), axis=1, keepdims=True), (128, 128)
    )

    scale = f32(1.0) / jnp.sqrt(f32(128.0))

    def attend(g, _):
        rows = pl.ds(pl.multiple_of(g * 16, 16), 16)
        qg = jnp.concatenate(
            [q[s, rows, h * 128 : (h + 1) * 128] for s in range(3) for h in range(4)], axis=0
        )
        kg = keys[rows].reshape(768, 128)
        vg = vals[rows].reshape(768, 128)
        nkg = jnp.concatenate([nk[s, rows, :] for s in range(3)], axis=0)
        nvg = jnp.concatenate([nv[s, rows, :] for s in range(3)], axis=0)
        bias = jnp.where(slotm[...].astype(f32) < lencol[rows, 0:1], 0.0, -1e30).astype(f32)
        s1 = (mm(qg, kg, NT) * scale).reshape(12, 16, 768) + bias[None]
        s1 = s1.reshape(192, 768)
        s2 = mm(qg, nkg, NT) * scale + freshb[...]
        top = jnp.maximum(jnp.max(s1, axis=1, keepdims=True), jnp.max(s2, axis=1, keepdims=True))
        e1 = jnp.exp(s1 - top)
        e2 = jnp.exp(s2 - top)
        inv = 1.0 / (jnp.sum(e1, axis=1, keepdims=True) + jnp.sum(e2, axis=1, keepdims=True))
        o = mm((e1 * inv).astype(bf16), vg) + mm((e2 * inv).astype(bf16), nvg)
        o = o.astype(bf16)
        for s in range(3):
            for h in range(4):
                i = (s * 4 + h) * 16
                att[s, rows, h * 128 : (h + 1) * 128] = o[i : i + 16]
        return 0

    for c in loads[4:9]:
        c.wait()
    lax.fori_loop(0, 2, attend, 0)

    drain(prs, r_prs)
    tot = part[t]
    for k in range(7):
        tot += prs[k]
    lows[...] = tot.astype(bf16)
    lowf[t] = tot.astype(bf16)

    def send_low(k, _):
        remote(lows, lowf.at[t], s_pag, r_pag, tpeer(k)).start()
        return 0

    lax.fori_loop(1, 8, send_low, 0)
    lax.fori_loop(2, 4, attend, 0)
    drain(lowf.at[pl.ds(0, 7)], r_pag)

    both = lowf[...].reshape(256, 128)
    both_t = both.astype(f32).T.astype(bf16)
    ga_t = mm(both_t[64:128], acts[...]).astype(bf16)
    gb = mm(both_t[0:64], cot[...]).astype(bf16)
    ga = mm(perma[...], ga_t, NT)
    gb = jnp.concatenate([gb[:, c * 128 : (c + 1) * 128] for c in range(5)], axis=0)
    gb = mm(spread[...], gb)
    gst[:, 0:16, :] = gb.astype(bf16).reshape(32, 16, 128)
    gst[:, 16:32, :] = jnp.concatenate([ga, jnp.zeros_like(ga)], axis=1).astype(bf16).reshape(32, 16, 128)
    cc = remote(gst.at[pl.ds((1 - core) * 16, 16)], gpeer, s_core, r_core, corepeer)
    cc.start()
    cc.wait_recv()
    hsum[...] = (gst[pl.ds(core * 16, 16)].astype(f32) + gpeer[...].astype(f32)).astype(bf16)

    def send_share(k, _):
        remote(hsum.at[(chip + k) % 16], hrecv.at[15 - k], s_dp, r_dp, cpeer(k)).start()
        return 0

    lax.fori_loop(1, 16, send_share, 0)
    lax.fori_loop(4, 8, attend, 0)
    attp[...] = mm(permr[...], att[...].reshape(384, 512)).astype(bf16)
    att2[...] = mm(attp[...], perma[...], NT).astype(bf16)
    drain(hrecv, r_dp)

    share = hsum[chip].astype(f32)
    for k in range(15):
        share += hrecv[k].astype(f32)
    share = share * (adapter_scale / 8192.0)
    gb_s[...] = share[0:16]
    ga_s[...] = share[16:32]
    for h in range(4):
        r = slice(h * 4, h * 4 + 4)
        new_p, new_m, new_v = adam_step(ma[h], oa[h], va[h], ga_s[r, 0:64])
        nma_o[h], noa_o[h], nva_o[h] = new_p, new_m, new_v
        ga_s[r, 0:64] = new_p
    for c in range(5):
        r = slice(c * 2, c * 2 + 2)
        l = slice(c * 128, (c + 1) * 128)
        new_p, new_m, new_v = adam_step(mb[:, l], ob[:, l], vb[:, l], gb_s[r, :])
        nmb_o[:, l], nob_o[:, l], nvb_o[:, l] = new_p, new_m, new_v
        gb_s[r, :] = new_p
    mine = core * 16 + chip
    fac[mine] = jnp.concatenate([gb_s[...], ga_s[...]], axis=0).astype(bf16)

    def send_fac(k, _):
        remote(fac.at[mine], fac.at[mine], s_fac, r_fac, cpeer(k)).start()
        return 0

    lax.fori_loop(1, 16, send_fac, 0)

    for c in loads[9:]:
        c.wait()

    def project(k, _):
        ysend[k - 1] = mm(attp[...], w[(t + k) % 8]).astype(bf16)
        remote(ysend.at[k - 1], yrecv.at[7 - k], s_y, r_y.at[7 - k], tpeer(k)).start()
        return 0

    lax.fori_loop(1, 8, project, 0)
    yown[...] = mm(attp[...], w[t])

    half = pl.ds(core * 16, 16)
    drain(fac.at[pl.ds(0, 15)], r_fac)
    fc = remote(fac.at[half], fac.at[half], s_fcore, r_fcore, corepeer)
    fc.start()
    thr = both[:, 64:128]
    add = [mm(thr, olda[h]) for h in range(4)]
    gacc[...] = adapter_scale * jnp.concatenate(add, axis=1) + mm(cot[...], w[t], NT)
    fc.wait_recv()

    a_new = fac[:, 16:32, :].reshape(512, 128)
    low = mm(att2[...], a_new)[:, 0:64]
    low = jnp.concatenate([low[0:192], low[192:384]], axis=1)
    lsend[...] = low.astype(bf16)

    def send_l(k, _):
        remote(lsend, lrecv.at[7 - k], s_low, r_low, tpeer(k)).start()
        return 0

    lax.fori_loop(1, 8, send_l, 0)
    b_new = mm(gather[...], fac[:, 0:16, :].reshape(512, 128)).astype(bf16)
    b_new = jnp.concatenate([b_new[c * 64 : (c + 1) * 64] for c in range(5)], axis=1)

    def accumulate(k, _):
        drain(cgat.at[7 - k], r_cot.at[7 - k])
        gacc[...] += mm(cgat[7 - k], w[(t + 8 - k) % 8], NT)
        return 0

    lax.fori_loop(1, 8, accumulate, 0)
    grad_o[...] = gacc[...].astype(bf16)

    drain(lrecv, r_low)
    for k in range(7):
        low += lrecv[k].astype(f32)
    low = jnp.concatenate([low[:, 0:64], low[:, 64:128]], axis=0)
    hi = low.astype(bf16)
    lo = (low - hi.astype(f32)).astype(bf16)
    yown[...] += adapter_scale * (mm(hi, b_new) + mm(lo, b_new))

    def collect(k, _):
        drain(yrecv.at[7 - k], r_y.at[7 - k])
        yown[...] += yrecv[7 - k].astype(f32)
        return 0

    lax.fori_loop(1, 8, collect, 0)
    out_o[...] = yown[...].T.astype(bf16)

    cc.wait_send()
    fc.wait_send()
    drain(prs, s_prs)
    drain(lowf.at[pl.ds(0, 7)], s_pag)
    drain(cgat, s_cot)
    drain(hrecv, s_dp)
    drain(fac.at[pl.ds(0, 15)], s_fac)
    drain(yrecv, s_y)
    drain(lrecv, s_low)


def per_device(
    acts, cotangent, out_weight, old_a, old_b, master_a, master_b, moment_a, moment_b, second_a, second_b,
    key_cache, value_cache, lengths, new_query, new_key, new_value,
):
    hbm = pl.BlockSpec(memory_space=pl.ANY)
    vmem = pl.BlockSpec(memory_space=pltpu.VMEM)
    dma = pltpu.SemaphoreType.DMA
    V = pltpu.VMEM
    shp = jax.ShapeDtypeStruct
    return pl.pallas_call(
        kernel,
        out_shape=(
            shp((256, 512), bf16), shp((4, 4, 64), f32), shp((2, 640), f32), shp((4, 4, 64), f32),
            shp((2, 640), f32), shp((4, 4, 64), f32), shp((2, 640), f32), shp((640, 384), bf16),
        ),
        in_specs=[hbm] * 5 + [vmem] * 6 + [hbm] * 2 + [vmem] + [hbm] * 3,
        out_specs=(vmem,) * 8,
        scratch_shapes=[
            V((256, 512), bf16), V((256, 640), bf16), V((8, 512, 640), bf16), V((4, 64, 128), bf16),
            V((64, 640), bf16), V((128, 48, 128), bf16), V((128, 48, 128), bf16), V((3, 128, 512), bf16),
            V((3, 128, 128), bf16), V((3, 128, 128), bf16),
            V((512, 512), bf16), V((512, 320), bf16), V((320, 512), bf16), V((384, 384), bf16),
            V((16, 768), jnp.int32), V((192, 48), f32), V((128, 128), f32),
            V((8, 32, 128), f32), V((7, 32, 128), f32), V((32, 128), bf16), V((8, 32, 128), bf16),
            V((7, 256, 640), bf16), V((256, 512), f32),
            V((32, 32, 128), bf16), V((16, 32, 128), bf16), V((16, 32, 128), bf16), V((15, 32, 128), bf16),
            V((16, 128), f32), V((16, 128), f32), V((32, 32, 128), bf16),
            V((3, 128, 512), bf16), V((384, 512), bf16), V((384, 512), bf16),
            V((7, 384, 640), bf16), V((384, 640), f32), V((7, 384, 640), bf16),
            V((192, 128), bf16), V((7, 192, 128), bf16),
            dma((17,)), dma, dma, dma, dma, dma, dma((7,)), dma, dma, dma, dma,
            dma, dma, dma, dma, dma, dma((7,)), dma, dma,
        ],
        compiler_params=pltpu.CompilerParams(
            collective_id=0, has_side_effects=True, vmem_limit_bytes=56 << 20
        ),
        cost_estimate=pl.CostEstimate(flops=4 << 30, bytes_accessed=12 << 20, transcendentals=1 << 20),
        name="update_and_decode",
    )(
        acts, cotangent, out_weight, old_a.swapaxes(1, 2), old_b,
        master_a, master_b, moment_a, moment_b, second_a, second_b,
        key_cache.reshape(128, 48, 128), value_cache.reshape(128, 48, 128), lengths.reshape(1, 128),
        new_query.swapaxes(0, 1), new_key.swapaxes(0, 1), new_value.swapaxes(0, 1),
    )


def solution(mesh):
    return jax.shard_map(
        per_device,
        mesh=mesh,
        in_specs=(
            P("dp", "tensor"),
            P("dp", "tensor"),
            P("tensor", None),
            P("tensor", None, None),
            P(),
            P("tensor", "dp", None),
            P("dp", "tensor"),
            P("tensor", "dp", None),
            P("dp", "tensor"),
            P("tensor", "dp", None),
            P("dp", "tensor"),
            P("dp", "tensor", None, None),
            P("dp", "tensor", None, None),
            P("dp"),
            P("dp", None, "tensor"),
            P("dp", None, "tensor"),
            P("dp", None, "tensor"),
        ),
        out_specs=(
            P("dp", "tensor"),
            P("tensor", "dp", None),
            P("dp", "tensor"),
            P("tensor", "dp", None),
            P("dp", "tensor"),
            P("tensor", "dp", None),
            P("dp", "tensor"),
            P("tensor", "dp"),
        ),
        check_vma=False,
    )
```

```python
import functools

import jax
import jax.numpy as jnp
from jax import lax
from jax.experimental import pallas as pl
from jax.experimental.pallas import tpu as pltpu
from jax.sharding import PartitionSpec as P

adapter_scale = 2.0
beta_one = 0.9
beta_two = 0.999
learn_rate = 0.01
decay_rate = 0.01
corr_one = 1.0 - 0.9**10
corr_two = 1.0 - 0.999**10
MESH = pl.DeviceIdType.MESH
f32 = jnp.float32
bf16 = jnp.bfloat16
NT = (((1,), (1,)), ((), ()))
NN = (((1,), (0,)), ((), ()))


def mm(a, b, dims=NN):
    return lax.dot_general(a, b, dims, preferred_element_type=f32)


def iota(shape, dim):
    return lax.broadcasted_iota(jnp.int32, shape, dim)


def onehot(hit):
    return jnp.where(hit, 1.0, 0.0).astype(f32).astype(bf16)


def adam_step(master, moment, second, grad):
    moment_new = beta_one * moment + (1.0 - beta_one) * grad
    second_new = beta_two * second + (1.0 - beta_two) * grad * grad
    update = moment_new / corr_one / (jnp.sqrt(second_new / corr_two) + 1e-08)
    return (master - learn_rate * (update + decay_rate * master), moment_new, second_new)


def kernel(
    acts_h, cot_h, w_h, olda_h, oldb_h,
    ma, mb, oa, ob, va, vb,
    key_h, val_h, len_ref, q_h, nk_h, nv_h,
    grad_o, nma_o, nmb_o, noa_o, nob_o, nva_o, nvb_o, out_o,
    acts, cot, w, olda, oldb, keys, vals, q, nk, nv,
    perma, spread, gather, permr, slotm, freshb, lencol,
    part, prs, lows, lowf, cgat, gacc,
    gst, gpeer, hsum, hrecv, ga_s, gb_s, fac,
    att, attp, att2, yb, yown, za, far, fin, zbr, lsend, lrecv,
    lsem, s_prs, r_prs, s_pag, r_pag, s_ag, r_ag, s_gz, r_gz, s_core, r_core, s_dp, r_dp,
    s_fac, r_fac, s_fcore, r_fcore, s_za, r_za, s_p1, r_p1, s_raw, r_raw, s_p2, r_p2, s_zb, r_zb, s_low, r_low,
):
    dp = lax.axis_index("dp")
    t = lax.axis_index("tensor")
    chip = dp // 2
    core = dp % 2
    z = t // 4
    y = t % 4

    def tpeer(k):
        return (dp, (t + k) % 8)

    def cpeer(k):
        return (((chip + k) % 16) * 2 + core, t)

    corepeer = (chip * 2 + 1 - core, t)
    twin = (1 - z) * 4 + y
    zdev = (dp, twin)
    ynext = ((y + 1) % 4, (y + 3) % 4)
    yfar = (y + 2) % 4
    ydev = tuple((dp, z * 4 + n) for n in ynext)
    yprev = (ynext[1], ynext[0])

    def remote(src, dst, ssem, rsem, dev):
        return pltpu.make_async_remote_copy(
            src_ref=src, dst_ref=dst, send_sem=ssem, recv_sem=rsem, device_id=dev, device_id_type=MESH
        )

    def drain(ref, sem):
        pltpu.make_async_copy(ref, ref, sem).wait()

    loads = [
        pltpu.make_async_copy(acts_h, acts, lsem.at[0]),
        pltpu.make_async_copy(cot_h, cot, lsem.at[1]),
        pltpu.make_async_copy(olda_h, olda, lsem.at[2]),
        pltpu.make_async_copy(oldb_h.at[:, pl.ds(pl.multiple_of(t * 640, 128), 640)], oldb, lsem.at[3]),
        pltpu.make_async_copy(q_h, q, lsem.at[4]),
        pltpu.make_async_copy(key_h, keys, lsem.at[5]),
        pltpu.make_async_copy(nk_h, nk, lsem.at[6]),
        pltpu.make_async_copy(val_h, vals, lsem.at[7]),
        pltpu.make_async_copy(nv_h, nv, lsem.at[8]),
    ]
    for j in range(8):
        loads.append(pltpu.make_async_copy(w_h.at[:, pl.ds(j * 640, 640)], w.at[j], lsem.at[9 + j]))
    for c in loads:
        c.start()

    bar = pltpu.get_barrier_semaphore()

    def sig_t(k, _):
        pl.semaphore_signal(bar, inc=1, device_id=tpeer(k), device_id_type=MESH)
        return 0

    def sig_c(k, _):
        pl.semaphore_signal(bar, inc=1, device_id=cpeer(k), device_id_type=MESH)
        return 0

    lax.fori_loop(1, 8, sig_t, 0)
    lax.fori_loop(1, 16, sig_c, 0)
    pl.semaphore_signal(bar, inc=1, device_id=corepeer, device_id_type=MESH)

    for c in loads[:4]:
        c.wait()
    low_p = mm(acts[:, 0:128], olda[0], NT)
    for h in range(1, 4):
        low_p += mm(acts[:, h * 128 : (h + 1) * 128], olda[h], NT)
    thr_p = mm(cot[...], oldb[...], NT)
    part[...] = jnp.concatenate([low_p, thr_p], axis=1).reshape(8, 32, 128)
    pl.semaphore_wait(bar, 23)

    def send_part(k, _):
        remote(part.at[(t + k) % 8], prs.at[7 - k], s_prs, r_prs, tpeer(k)).start()
        return 0

    lax.fori_loop(1, 8, send_part, 0)

    def half(h):
        return pl.ds(h * 128, 128)

    def gather_own(h):
        remote(cot.at[half(h)], cgat.at[t, half(h)], s_gz, r_gz.at[h], zdev).start()
        for d in range(2):
            remote(cot.at[half(h)], cgat.at[t, half(h)], s_ag, r_ag.at[d, h], ydev[d]).start()

    def gather_twin(h):
        drain(cgat.at[twin, half(h)], r_gz.at[h])
        for d in range(2):
            remote(cgat.at[twin, half(h)], cgat.at[twin, half(h)], s_ag, r_ag.at[d, 2 + h], ydev[d]).start()

    def gather_relay(which):
        for d in range(2):
            src = (z if which == 0 else 1 - z) * 4 + yprev[d]
            blk = cgat.at[src, half(d)]
            drain(blk, r_ag.at[d, which * 2 + d])
            remote(blk, blk, s_ag, r_ag.at[d, 4 + which], ydev[d]).start()

    gather_own(0)

    prow, pcol = iota((512, 512), 0), iota((512, 512), 1)
    blk = prow >> 4
    perma[...] = onehot(
        pcol == (((prow >> 2) & 3) << 7) + (((blk & 15) * 2 + (blk >> 4)) << 2) + (prow & 3)
    )
    erow, ecol = iota((512, 320), 0), iota((512, 320), 1)
    blk = erow >> 4
    idx = erow & 15
    spread[...] = onehot(
        (idx < 10) & (ecol == ((idx >> 1) << 6) + ((blk & 15) * 2 + (blk >> 4)) * 2 + (idx & 1))
    )
    erow, ecol = iota((320, 512), 1), iota((320, 512), 0)
    blk = erow >> 4
    idx = erow & 15
    gather[...] = onehot(
        (idx < 10) & (ecol == ((idx >> 1) << 6) + ((blk & 15) * 2 + (blk >> 4)) * 2 + (idx & 1))
    )
    rj, rk = iota((192, 192), 0), iota((192, 192), 1)
    permr[...] = onehot((rj - 3 * (rk & 63)) == (rk >> 6))
    slot = iota((16, 768), 1) - 48 * iota((16, 768), 0)
    slotm[...] = jnp.where((slot >= 0) & (slot < 48), slot, 1000)
    fr, fc = iota((192, 48), 0), iota((192, 48), 1)
    freshb[...] = jnp.where(((fr & 15) == (fc & 15)) & ((fc >> 4) <= (fr >> 6)), 0.0, -1e30).astype(f32)
    diag = iota((128, 128), 0) == iota((128, 128), 1)
    lencol[...] = jnp.broadcast_to(
        jnp.sum(jnp.where(diag, len_ref[...].astype(f32), 0.0), axis=1, keepdims=True), (128, 128)
    )

    scale = f32(1.0) / jnp.sqrt(f32(128.0))

    def attend(g, _):
        rows = pl.ds(pl.multiple_of(g * 16, 16), 16)
        qg = jnp.concatenate(
            [q[s, rows, h * 128 : (h + 1) * 128] for s in range(3) for h in range(4)], axis=0
        )
        kg = keys[rows].reshape(768, 128)
        vg = vals[rows].reshape(768, 128)
        nkg = jnp.concatenate([nk[s, rows, :] for s in range(3)], axis=0)
        nvg = jnp.concatenate([nv[s, rows, :] for s in range(3)], axis=0)
        bias = jnp.where(slotm[...].astype(f32) < lencol[rows, 0:1], 0.0, -1e30).astype(f32)
        s1 = (mm(qg, kg, NT) * scale).reshape(12, 16, 768) + bias[None]
        s1 = s1.reshape(192, 768)
        s2 = mm(qg, nkg, NT) * scale + freshb[...]
        top = jnp.maximum(jnp.max(s1, axis=1, keepdims=True), jnp.max(s2, axis=1, keepdims=True))
        e1 = jnp.exp(s1 - top)
        e2 = jnp.exp(s2 - top)
        inv = 1.0 / (jnp.sum(e1, axis=1, keepdims=True) + jnp.sum(e2, axis=1, keepdims=True))
        o = mm((e1 * inv).astype(bf16), vg) + mm((e2 * inv).astype(bf16), nvg)
        o = o.astype(bf16)
        for s in range(3):
            for h in range(4):
                i = (s * 4 + h) * 16
                att[s, rows, h * 128 : (h + 1) * 128] = o[i : i + 16]
        return 0

    rows_a = pl.ds(0, 192)
    rows_b = pl.ds(192, 192)

    def order_rows(i):
        block = att[:, i * 64 : (i + 1) * 64, :].reshape(192, 512)
        attp[pl.ds(i * 192, 192)] = mm(permr[...], block).astype(bf16)

    def project(rows):
        def one(j, _):
            yb[j, rows] = mm(attp[rows], w[j]).astype(bf16)
            return 0

        return one

    this, other = z * 4, (1 - z) * 4

    def send_za(j):
        remote(yb.at[other + j, rows_a], za.at[j], s_za, r_za.at[j], zdev).start()

    half_rows = 96
    classes = ((0, z), (192, z), (192, 1 - z))

    def part_of(c, owner, h):
        r0, plane = classes[c]
        return yb.at[plane * 4 + owner, pl.ds(r0 + h * half_rows, half_rows)]

    def y_far(c):
        for d in range(2):
            remote(part_of(c, yfar, d), far.at[c, d], s_p1.at[c], r_p1.at[c, d], ydev[d]).start()

    def y_raw(c):
        for d in range(2):
            remote(
                part_of(c, ynext[d], 1 - d), fin.at[c, d, 1 - d], s_raw.at[c], r_raw.at[c, d], ydev[d]
            ).start()

    def y_relay(c):
        for d in range(2):
            drain(far.at[c, d], r_p1.at[c, d])
            blk = part_of(c, ynext[d], d)
            blk[...] = (blk[...].astype(f32) + far[c, d].astype(f32)).astype(bf16)
            remote(blk, fin.at[c, d, d], s_p2.at[c], r_p2.at[c, d], ydev[d]).start()

    def y_total(c, h):
        return fin[c, 0, h].astype(f32) + fin[c, 1, h].astype(f32)

    def y_wait(c):
        for d in range(2):
            drain(fin.at[c, d, 1 - d], r_raw.at[c, d])
            drain(fin.at[c, d, d], r_p2.at[c, d])

    for c in loads[4:9]:
        c.wait()
    lax.fori_loop(0, 4, attend, 0)
    order_rows(0)

    drain(prs, r_prs)
    tot = part[t]
    for k in range(7):
        tot += prs[k]
    lows[...] = tot.astype(bf16)
    lowf[t] = tot.astype(bf16)

    def send_low(k, _):
        remote(lows, lowf.at[t], s_pag, r_pag, tpeer(k)).start()
        return 0

    lax.fori_loop(1, 8, send_low, 0)
    gather_own(1)
    for c in loads[9:]:
        c.wait()
    lax.fori_loop(other, other + 4, project(rows_a), 0)
    send_za(0)
    gather_twin(0)
    lax.fori_loop(4, 6, attend, 0)

    drain(lowf.at[pl.ds(0, 7)], r_pag)

    both = lowf[...].reshape(256, 128)
    both_t = both.astype(f32).T.astype(bf16)
    ga_t = mm(both_t[64:128], acts[...]).astype(bf16)
    gb = mm(both_t[0:64], cot[...]).astype(bf16)
    ga = mm(perma[...], ga_t, NT)
    gb = jnp.concatenate([gb[:, c * 128 : (c + 1) * 128] for c in range(5)], axis=0)
    gb = mm(spread[...], gb)
    gst[:, 0:16, :] = gb.astype(bf16).reshape(32, 16, 128)
    gst[:, 16:32, :] = jnp.concatenate([ga, jnp.zeros_like(ga)], axis=1).astype(bf16).reshape(32, 16, 128)
    cc = remote(gst.at[pl.ds((1 - core) * 16, 16)], gpeer, s_core, r_core, corepeer)
    cc.start()

    lax.fori_loop(6, 8, attend, 0)
    cc.wait_recv()
    hsum[...] = (gst[pl.ds(core * 16, 16)].astype(f32) + gpeer[...].astype(f32)).astype(bf16)

    def send_share(k, _):
        remote(hsum.at[(chip + k) % 16], hrecv.at[15 - k], s_dp, r_dp, cpeer(k)).start()
        return 0

    lax.fori_loop(1, 16, send_share, 0)
    gather_twin(1)
    send_za(1)
    order_rows(1)
    lax.fori_loop(other, other + 4, project(rows_b), 0)
    lax.fori_loop(this, this + 4, project(rows_b), 0)
    gather_relay(0)
    y_far(2)
    y_far(1)
    lax.fori_loop(this, this + 4, project(rows_a), 0)
    yown[...] = mm(attp[...], w[t])
    att2[...] = mm(attp[...], perma[...], NT).astype(bf16)

    drain(hrecv, r_dp)

    share = hsum[chip].astype(f32)
    for k in range(15):
        share += hrecv[k].astype(f32)
    share = share * (adapter_scale / 8192.0)
    gb_s[...] = share[0:16]
    ga_s[...] = share[16:32]
    for h in range(4):
        r = slice(h * 4, h * 4 + 4)
        new_p, new_m, new_v = adam_step(ma[h], oa[h], va[h], ga_s[r, 0:64])
        nma_o[h], noa_o[h], nva_o[h] = new_p, new_m, new_v
        ga_s[r, 0:64] = new_p
    for c in range(5):
        r = slice(c * 2, c * 2 + 2)
        l = slice(c * 128, (c + 1) * 128)
        new_p, new_m, new_v = adam_step(mb[:, l], ob[:, l], vb[:, l], gb_s[r, :])
        nmb_o[:, l], nob_o[:, l], nvb_o[:, l] = new_p, new_m, new_v
        gb_s[r, :] = new_p
    mine = core * 16 + chip
    fac[mine] = jnp.concatenate([gb_s[...], ga_s[...]], axis=0).astype(bf16)

    def send_fac(k, _):
        remote(fac.at[mine], fac.at[mine], s_fac, r_fac, cpeer(k)).start()
        return 0

    lax.fori_loop(1, 16, send_fac, 0)
    send_za(2)
    send_za(3)
    gather_relay(1)

    thr = both[:, 64:128]
    add = [mm(thr, olda[h]) for h in range(4)]
    gacc[...] = adapter_scale * jnp.concatenate(add, axis=1) + mm(cot[...], w[t], NT)
    gacc[...] += mm(cgat[twin], w[twin], NT)

    y_relay(2)
    y_raw(2)
    y_relay(1)

    mycore = pl.ds(core * 16, 16)
    drain(fac.at[pl.ds(0, 15)], r_fac)
    fc = remote(fac.at[mycore], fac.at[mycore], s_fcore, r_fcore, corepeer)
    fc.start()
    fc.wait_recv()

    a_new = fac[:, 16:32, :].reshape(512, 128)
    low = mm(att2[...], a_new)[:, 0:64]
    low = jnp.concatenate([low[0:192], low[192:384]], axis=1)
    lsend[...] = low.astype(bf16)

    def send_l(k, _):
        remote(lsend, lrecv.at[7 - k], s_low, r_low, tpeer(k)).start()
        return 0

    lax.fori_loop(1, 8, send_l, 0)
    b_new = mm(gather[...], fac[:, 0:16, :].reshape(512, 128)).astype(bf16)
    b_new = jnp.concatenate([b_new[c * 64 : (c + 1) * 64] for c in range(5)], axis=1)

    for j in range(4):
        drain(za.at[j], r_za.at[j])
        blk = yb.at[this + j, rows_a]
        blk[...] = (blk[...].astype(f32) + za[j].astype(f32)).astype(bf16)
    yown[rows_a] += za[y].astype(f32)
    y_far(0)
    y_raw(1)

    for d in range(2):
        for h in range(2):
            if h != d:
                drain(cgat.at[this + yprev[d], half(h)], r_ag.at[d, h])
                drain(cgat.at[other + yprev[d], half(h)], r_ag.at[d, 2 + h])
        drain(cgat.at[this + yfar, half(d)], r_ag.at[d, 4])
        drain(cgat.at[other + yfar, half(d)], r_ag.at[d, 5])

    def accumulate(k, _):
        src = jnp.where(k < 3, z, 1 - z) * 4 + (y + 1 + k % 3) % 4
        gacc[...] += mm(cgat[src], w[src], NT)
        return 0

    lax.fori_loop(0, 6, accumulate, 0)
    grad_o[...] = gacc[...].astype(bf16)

    y_wait(2)
    for h in range(2):
        blk = part_of(2, y, h)
        blk[...] = (blk[...].astype(f32) + y_total(2, h)).astype(bf16)
    zb = remote(yb.at[twin, rows_b], zbr, s_zb, r_zb, zdev)
    zb.start()

    y_relay(0)
    y_raw(0)

    drain(lrecv, r_low)
    for k in range(7):
        low += lrecv[k].astype(f32)
    low = jnp.concatenate([low[:, 0:64], low[:, 64:128]], axis=0)
    hi = low.astype(bf16)
    lo = (low - hi.astype(f32)).astype(bf16)
    yown[...] += adapter_scale * (mm(hi, b_new) + mm(lo, b_new))

    y_wait(1)
    for h in range(2):
        yown[pl.ds(192 + h * half_rows, half_rows)] += y_total(1, h)
    zb.wait_recv()
    yown[rows_b] += zbr[...].astype(f32)
    y_wait(0)
    for h in range(2):
        yown[pl.ds(h * half_rows, half_rows)] += y_total(0, h)
    out_o[...] = yown[...].T.astype(bf16)

    cc.wait_send()
    fc.wait_send()
    zb.wait_send()
    drain(prs, s_prs)
    drain(lowf.at[pl.ds(0, 7)], s_pag)
    drain(cgat.at[0], s_gz)
    drain(cgat.at[pl.ds(0, 6)], s_ag)
    drain(hrecv, s_dp)
    drain(fac.at[pl.ds(0, 15)], s_fac)
    drain(za, s_za)
    for c in range(3):
        for sem in (s_p1, s_raw, s_p2):
            drain(far.at[c], sem.at[c])
    drain(lrecv, s_low)


def hand_over(*refs):
    n = len(refs) // 2
    for i in range(n):
        refs[n + i][...] = refs[i][...]


def per_device(
    acts, cotangent, out_weight, old_a, old_b, master_a, master_b, moment_a, moment_b, second_a, second_b,
    key_cache, value_cache, lengths, new_query, new_key, new_value,
):
    hbm = pl.BlockSpec(memory_space=pl.ANY)
    vmem = pl.BlockSpec(memory_space=pltpu.VMEM)
    dma = pltpu.SemaphoreType.DMA
    V = pltpu.VMEM
    shp = jax.ShapeDtypeStruct
    results = pl.pallas_call(
        kernel,
        out_shape=(
            shp((256, 512), bf16), shp((4, 4, 64), f32), shp((2, 640), f32), shp((4, 4, 64), f32),
            shp((2, 640), f32), shp((4, 4, 64), f32), shp((2, 640), f32), shp((640, 384), bf16),
        ),
        in_specs=[hbm] * 5 + [vmem] * 6 + [hbm] * 2 + [vmem] + [hbm] * 3,
        out_specs=(vmem,) * 8,
        scratch_shapes=[
            V((256, 512), bf16), V((256, 640), bf16), V((8, 512, 640), bf16), V((4, 64, 128), bf16),
            V((64, 640), bf16), V((128, 48, 128), bf16), V((128, 48, 128), bf16), V((3, 128, 512), bf16),
            V((3, 128, 128), bf16), V((3, 128, 128), bf16),
            V((512, 512), bf16), V((512, 320), bf16), V((320, 512), bf16), V((192, 192), bf16),
            V((16, 768), jnp.int32), V((192, 48), f32), V((128, 128), f32),
            V((8, 32, 128), f32), V((7, 32, 128), f32), V((32, 128), bf16), V((8, 32, 128), bf16),
            V((8, 256, 640), bf16), V((256, 512), f32),
            V((32, 32, 128), bf16), V((16, 32, 128), bf16), V((16, 32, 128), bf16), V((15, 32, 128), bf16),
            V((16, 128), f32), V((16, 128), f32), V((32, 32, 128), bf16),
            V((3, 128, 512), bf16), V((384, 512), bf16), V((384, 512), bf16),
            V((8, 384, 640), bf16), V((384, 640), f32), V((4, 192, 640), bf16),
            V((3, 2, 96, 640), bf16), V((3, 2, 2, 96, 640), bf16), V((192, 640), bf16), V((192, 128), bf16), V((7, 192, 128), bf16),
            dma((17,)), dma, dma, dma, dma, dma, dma((2, 6)), dma, dma((2,)), dma, dma, dma, dma,
            dma, dma, dma, dma, dma, dma((4,)), dma((3,)), dma((3, 2)), dma((3,)), dma((3, 2)), dma((3,)), dma((3, 2)),
            dma, dma, dma, dma,
        ],
        compiler_params=pltpu.CompilerParams(
            collective_id=0, has_side_effects=True, vmem_limit_bytes=56 << 20
        ),
        cost_estimate=pl.CostEstimate(flops=4 << 30, bytes_accessed=12 << 20, transcendentals=1 << 20),
        name="update_and_decode",
    )(
        acts, cotangent, out_weight, old_a.swapaxes(1, 2), old_b,
        master_a, master_b, moment_a, moment_b, second_a, second_b,
        key_cache.reshape(128, 48, 128), value_cache.reshape(128, 48, 128), lengths.reshape(1, 128),
        new_query.swapaxes(0, 1), new_key.swapaxes(0, 1), new_value.swapaxes(0, 1),
    )
    return pl.pallas_call(
        hand_over,
        out_shape=tuple(shp(r.shape, r.dtype) for r in results),
        in_specs=[vmem] * 8,
        out_specs=(vmem,) * 8,
        cost_estimate=pl.CostEstimate(flops=0, bytes_accessed=2 << 20, transcendentals=0),
        name="hand_over",
    )(*results)


def solution(mesh):
    return jax.shard_map(
        per_device,
        mesh=mesh,
        in_specs=(
            P("dp", "tensor"),
            P("dp", "tensor"),
            P("tensor", None),
            P("tensor", None, None),
            P(),
            P("tensor", "dp", None),
            P("dp", "tensor"),
            P("tensor", "dp", None),
            P("dp", "tensor"),
            P("tensor", "dp", None),
            P("dp", "tensor"),
            P("dp", "tensor", None, None),
            P("dp", "tensor", None, None),
            P("dp"),
            P("dp", None, "tensor"),
            P("dp", None, "tensor"),
            P("dp", None, "tensor"),
        ),
        out_specs=(
            P("dp", "tensor"),
            P("tensor", "dp", None),
            P("dp", "tensor"),
            P("tensor", "dp", None),
            P("dp", "tensor"),
            P("tensor", "dp", None),
            P("dp", "tensor"),
            P("tensor", "dp"),
        ),
        check_vma=False,
    )
```

```python
import functools

import jax
import jax.numpy as jnp
from jax import lax
from jax.experimental import pallas as pl
from jax.experimental.pallas import tpu as pltpu
from jax.sharding import PartitionSpec as P

adapter_scale = 2.0
beta_one = 0.9
beta_two = 0.999
learn_rate = 0.01
decay_rate = 0.01
corr_one = 1.0 - 0.9**10
corr_two = 1.0 - 0.999**10
MESH = pl.DeviceIdType.MESH
f32 = jnp.float32
bf16 = jnp.bfloat16
NT = (((1,), (1,)), ((), ()))
NN = (((1,), (0,)), ((), ()))


def mm(a, b, dims=NN):
    return lax.dot_general(a, b, dims, preferred_element_type=f32)


def iota(shape, dim):
    return lax.broadcasted_iota(jnp.int32, shape, dim)


def onehot(hit):
    return jnp.where(hit, 1.0, 0.0).astype(f32).astype(bf16)


def adam_step(master, moment, second, grad):
    moment_new = beta_one * moment + (1.0 - beta_one) * grad
    second_new = beta_two * second + (1.0 - beta_two) * grad * grad
    update = moment_new / corr_one / (jnp.sqrt(second_new / corr_two) + 1e-08)
    return (master - learn_rate * (update + decay_rate * master), moment_new, second_new)


def kernel(
    acts_h, cot_h, w_h, olda_h, oldb_h,
    ma_h, mb_h, oa_h, ob_h, va_h, vb_h,
    key_h, val_h, len_h, q_h, nk_h, nv_h,
    grad_o, nma_o, nmb_o, noa_o, nob_o, nva_o, nvb_o, out_o,
    acts, cot, w, olda, oldb, keys, vals, q, nk, nv,
    ma, mb, oa, ob, va, vb, len_ref,
    perma, spread, gather, permr, slotm, freshb, lencol,
    part, prs, lows, lowf, cgat, gacc,
    gst, gpeer, hsum, xrecv, xsum, zrecv, ga_s, gb_s, fac,
    att, attp, att2, yb, yown, za, far, fin, zbr, lsend, lpeer, lrecv,
    lsem, s_prs, r_prs, s_pag, r_pag, s_ag, r_ag, s_gz, r_gz, s_gb, s_gbz, s_core, r_core, s_dx, r_dx, s_dz, r_dz,
    s_fz, r_fz, s_fx, r_fx, s_fcore, r_fcore, s_za, r_za, s_p1, r_p1, s_raw, r_raw, s_p2, r_p2, s_zb, r_zb, s_lz, r_lz, s_low, r_low,
):
    dp = lax.axis_index("dp")
    t = lax.axis_index("tensor")
    chip = dp // 2
    core = dp % 2
    z = t // 4
    y = t % 4

    def tpeer(k):
        return (dp, (t + k) % 8)

    cx, cz = chip // 4, chip % 4

    def xpeer(k):
        return ((((cx + k) % 4) * 4 + cz) * 2 + core, t)

    def zpeer(k):
        return ((cx * 4 + (cz + k) % 4) * 2 + core, t)

    corepeer = (chip * 2 + 1 - core, t)
    twin = (1 - z) * 4 + y
    zdev = (dp, twin)
    ynext = ((y + 1) % 4, (y + 3) % 4)
    yfar = (y + 2) % 4
    ydev = tuple((dp, z * 4 + n) for n in ynext)
    yprev = (ynext[1], ynext[0])

    def remote(src, dst, ssem, rsem, dev):
        return pltpu.make_async_remote_copy(
            src_ref=src, dst_ref=dst, send_sem=ssem, recv_sem=rsem, device_id=dev, device_id_type=MESH
        )

    def drain(ref, sem):
        pltpu.make_async_copy(ref, ref, sem).wait()

    loads = [
        pltpu.make_async_copy(acts_h, acts, lsem.at[0]),
        pltpu.make_async_copy(cot_h, cot, lsem.at[1]),
        pltpu.make_async_copy(olda_h, olda, lsem.at[2]),
        pltpu.make_async_copy(oldb_h.at[:, pl.ds(pl.multiple_of(t * 640, 128), 640)], oldb, lsem.at[3]),
        pltpu.make_async_copy(q_h, q, lsem.at[4]),
        pltpu.make_async_copy(key_h, keys, lsem.at[5]),
        pltpu.make_async_copy(nk_h, nk, lsem.at[6]),
        pltpu.make_async_copy(val_h, vals, lsem.at[7]),
        pltpu.make_async_copy(nv_h, nv, lsem.at[8]),
    ]
    for j in range(8):
        loads.append(pltpu.make_async_copy(w_h.at[:, pl.ds(j * 640, 640)], w.at[j], lsem.at[9 + j]))
    small = ((len_h, len_ref), (ma_h, ma), (mb_h, mb), (oa_h, oa), (ob_h, ob), (va_h, va), (vb_h, vb))
    state = [pltpu.make_async_copy(a, b, lsem.at[17 + i]) for i, (a, b) in enumerate(small)]
    for c in loads + state:
        c.start()

    bar = pltpu.get_barrier_semaphore()

    def sig_t(k, _):
        pl.semaphore_signal(bar, inc=1, device_id=tpeer(k), device_id_type=MESH)
        return 0

    def sig_c(k, _):
        pl.semaphore_signal(bar, inc=1, device_id=xpeer(k), device_id_type=MESH)
        pl.semaphore_signal(bar, inc=1, device_id=zpeer(k), device_id_type=MESH)
        return 0

    lax.fori_loop(1, 8, sig_t, 0)
    lax.fori_loop(1, 4, sig_c, 0)
    pl.semaphore_signal(bar, inc=1, device_id=corepeer, device_id_type=MESH)

    for c in loads[:4]:
        c.wait()
    low_p = mm(acts[:, 0:128], olda[0], NT)
    for h in range(1, 4):
        low_p += mm(acts[:, h * 128 : (h + 1) * 128], olda[h], NT)
    thr_p = mm(cot[...], oldb[...], NT)
    part[...] = jnp.concatenate([low_p, thr_p], axis=1).reshape(8, 32, 128)
    pl.semaphore_wait(bar, 14)

    def send_part(k, _):
        remote(part.at[(t + k) % 8], prs.at[7 - k], s_prs, r_prs, tpeer(k)).start()
        return 0

    lax.fori_loop(1, 8, send_part, 0)

    gather_b = pl.ds(0, 64)

    def b_half(h):
        return pl.ds(h * 32, 32)

    def a_half(h):
        return pl.ds(64 + h * 96, 96)

    def gather_own(h):
        remote(cot.at[a_half(h)], cgat.at[t, a_half(h)], s_gz, r_gz.at[h], zdev).start()
        for d in range(2):
            remote(cot.at[a_half(h)], cgat.at[t, a_half(h)], s_ag, r_ag.at[d, 1 + h], ydev[d]).start()

    def gather_twin(h):
        blk = cgat.at[twin, a_half(h)]
        drain(blk, r_gz.at[h])
        for d in range(2):
            remote(blk, blk, s_ag, r_ag.at[d, 3 + h], ydev[d]).start()

    def gather_relay(which):
        for d in range(2):
            blk = cgat.at[(z if which == 0 else 1 - z) * 4 + yprev[d], a_half(d)]
            drain(blk, r_ag.at[d, 1 + which * 2 + d])
            remote(blk, blk, s_ag, r_ag.at[d, 6 + which], ydev[d]).start()

    def gather_b_own():
        for d in range(2):
            remote(cot.at[gather_b], cgat.at[t, gather_b], s_gb, r_ag.at[d, 0], ydev[d]).start()

    def gather_b_relay():
        for d in range(2):
            drain(cgat.at[z * 4 + yprev[d], gather_b], r_ag.at[d, 0])
            blk = cgat.at[z * 4 + yprev[d], b_half(d)]
            remote(blk, blk, s_gb, r_ag.at[d, 5], ydev[d]).start()

    def gather_b_twin():
        remote(cot.at[gather_b], cgat.at[t, gather_b], s_gbz, r_gz.at[2], zdev).start()

    def gather_b_next():
        for d in range(2):
            blk = cgat.at[z * 4 + yprev[d], gather_b]
            remote(blk, blk, s_gbz, r_gz.at[3 + d], zdev).start()

    def gather_b_far():
        for d in range(2):
            drain(cgat.at[z * 4 + yfar, b_half(d)], r_ag.at[d, 5])
        blk = cgat.at[z * 4 + yfar, gather_b]
        remote(blk, blk, s_gbz, r_gz.at[5], zdev).start()

    gather_b_own()
    gather_own(0)
    gather_b_twin()

    prow, pcol = iota((512, 512), 0), iota((512, 512), 1)
    blk = prow >> 4
    perma[...] = onehot(
        pcol == (((prow >> 2) & 3) << 7) + (((blk & 15) * 2 + (blk >> 4)) << 2) + (prow & 3)
    )
    erow, ecol = iota((512, 320), 0), iota((512, 320), 1)
    blk = erow >> 4
    idx = erow & 15
    spread[...] = onehot(
        (idx < 10) & (ecol == ((idx >> 1) << 6) + ((blk & 15) * 2 + (blk >> 4)) * 2 + (idx & 1))
    )
    erow, ecol = iota((320, 512), 1), iota((320, 512), 0)
    blk = erow >> 4
    idx = erow & 15
    gather[...] = onehot(
        (idx < 10) & (ecol == ((idx >> 1) << 6) + ((blk & 15) * 2 + (blk >> 4)) * 2 + (idx & 1))
    )
    rj, rk = iota((192, 192), 0), iota((192, 192), 1)
    permr[...] = onehot((rj - 3 * (rk & 63)) == (rk >> 6))
    slot = iota((16, 768), 1) - 48 * iota((16, 768), 0)
    slotm[...] = jnp.where((slot >= 0) & (slot < 48), slot, 1000)
    fr, fc = iota((192, 48), 0), iota((192, 48), 1)
    freshb[...] = jnp.where(((fr & 15) == (fc & 15)) & ((fc >> 4) <= (fr >> 6)), 0.0, -1e30).astype(f32)
    state[0].wait()
    diag = iota((128, 128), 0) == iota((128, 128), 1)
    lencol[...] = jnp.broadcast_to(
        jnp.sum(jnp.where(diag, len_ref[...].astype(f32), 0.0), axis=1, keepdims=True), (128, 128)
    )

    scale = f32(1.0) / jnp.sqrt(f32(128.0))

    def attend(g, _):
        rows = pl.ds(pl.multiple_of(g * 16, 16), 16)
        qg = jnp.concatenate(
            [q[s, rows, h * 128 : (h + 1) * 128] for s in range(3) for h in range(4)], axis=0
        )
        kg = keys[rows].reshape(768, 128)
        vg = vals[rows].reshape(768, 128)
        nkg = jnp.concatenate([nk[s, rows, :] for s in range(3)], axis=0)
        nvg = jnp.concatenate([nv[s, rows, :] for s in range(3)], axis=0)
        bias = jnp.where(slotm[...].astype(f32) < lencol[rows, 0:1], 0.0, -1e30).astype(f32)
        s1 = (mm(qg, kg, NT) * scale).reshape(12, 16, 768) + bias[None]
        s1 = s1.reshape(192, 768)
        s2 = mm(qg, nkg, NT) * scale + freshb[...]
        top = jnp.maximum(jnp.max(s1, axis=1, keepdims=True), jnp.max(s2, axis=1, keepdims=True))
        e1 = jnp.exp(s1 - top)
        e2 = jnp.exp(s2 - top)
        inv = 1.0 / (jnp.sum(e1, axis=1, keepdims=True) + jnp.sum(e2, axis=1, keepdims=True))
        o = mm((e1 * inv).astype(bf16), vg) + mm((e2 * inv).astype(bf16), nvg)
        o = o.astype(bf16)
        for s in range(3):
            for h in range(4):
                i = (s * 4 + h) * 16
                att[s, rows, h * 128 : (h + 1) * 128] = o[i : i + 16]
        return 0

    rows_a = pl.ds(0, 192)
    rows_b = pl.ds(192, 192)

    def order_rows(i):
        block = att[:, i * 64 : (i + 1) * 64, :].reshape(192, 512)
        attp[pl.ds(i * 192, 192)] = mm(permr[...], block).astype(bf16)

    def project(rows):
        def one(j, _):
            yb[j, rows] = mm(attp[rows], w[j]).astype(bf16)
            return 0

        return one

    this, other = z * 4, (1 - z) * 4

    def send_za(j):
        remote(yb.at[other + j, rows_a], za.at[j], s_za, r_za.at[j], zdev).start()

    half_rows = 96
    classes = ((0, z), (192, z), (192, 1 - z))

    def part_of(c, owner, h):
        r0, plane = classes[c]
        return yb.at[plane * 4 + owner, pl.ds(r0 + h * half_rows, half_rows)]

    def y_far(c):
        for d in range(2):
            remote(part_of(c, yfar, d), far.at[c, d], s_p1.at[c], r_p1.at[c, d], ydev[d]).start()

    def y_raw(c):
        for d in range(2):
            remote(
                part_of(c, ynext[d], 1 - d), fin.at[c, d, 1 - d], s_raw.at[c], r_raw.at[c, d], ydev[d]
            ).start()

    def y_relay(c):
        for d in range(2):
            drain(far.at[c, d], r_p1.at[c, d])
            blk = part_of(c, ynext[d], d)
            blk[...] = (blk[...].astype(f32) + far[c, d].astype(f32)).astype(bf16)
            remote(blk, fin.at[c, d, d], s_p2.at[c], r_p2.at[c, d], ydev[d]).start()

    def y_total(c, h):
        return fin[c, 0, h].astype(f32) + fin[c, 1, h].astype(f32)

    def y_wait(c):
        for d in range(2):
            drain(fin.at[c, d, 1 - d], r_raw.at[c, d])
            drain(fin.at[c, d, d], r_p2.at[c, d])

    for c in loads[4:9]:
        c.wait()
    lax.fori_loop(0, 4, attend, 0)
    order_rows(0)

    drain(prs, r_prs)
    tot = part[t]
    for k in range(7):
        tot += prs[k]
    lows[...] = tot.astype(bf16)
    lowf[t] = tot.astype(bf16)

    def send_low(k, _):
        remote(lows, lowf.at[t], s_pag, r_pag, tpeer(k)).start()
        return 0

    lax.fori_loop(1, 8, send_low, 0)
    gather_own(1)
    for c in loads[9:]:
        c.wait()
    lax.fori_loop(other, other + 4, project(rows_a), 0)
    gather_b_relay()
    gather_twin(0)
    gather_b_next()
    lax.fori_loop(4, 6, attend, 0)

    drain(lowf.at[pl.ds(0, 7)], r_pag)

    both = lowf[...].reshape(256, 128)
    both_t = both.astype(f32).T.astype(bf16)
    ga_t = mm(both_t[64:128], acts[...]).astype(bf16)
    gb = mm(both_t[0:64], cot[...]).astype(bf16)
    ga = mm(perma[...], ga_t, NT)
    gb = jnp.concatenate([gb[:, c * 128 : (c + 1) * 128] for c in range(5)], axis=0)
    gb = mm(spread[...], gb)
    gst[:, 0:16, :] = gb.astype(bf16).reshape(32, 16, 128)
    gst[:, 16:32, :] = jnp.concatenate([ga, jnp.zeros_like(ga)], axis=1).astype(bf16).reshape(32, 16, 128)
    cc = remote(gst.at[pl.ds((1 - core) * 16, 16)], gpeer, s_core, r_core, corepeer)
    cc.start()

    lax.fori_loop(6, 8, attend, 0)
    gather_twin(1)
    gather_relay(0)
    cc.wait_recv()
    hsum[...] = (gst[pl.ds(core * 16, 16)].astype(f32) + gpeer[...].astype(f32)).astype(bf16)

    for k in range(1, 4):
        remote(hsum.at[pl.ds((cx + k) % 4 * 4, 4)], xrecv.at[3 - k], s_dx, r_dx, xpeer(k)).start()
    send_za(yfar)
    order_rows(1)
    lax.fori_loop(other, other + 4, project(rows_b), 0)
    y_far(2)
    lax.fori_loop(this, this + 4, project(rows_b), 0)
    y_far(1)
    drain(xrecv, r_dx)
    xtot = hsum[pl.ds(cx * 4, 4)].astype(f32)
    for k in range(3):
        xtot += xrecv[k].astype(f32)
    xsum[...] = xtot.astype(bf16)
    for k in range(1, 4):
        remote(xsum.at[(cz + k) % 4], zrecv.at[3 - k], s_dz, r_dz, zpeer(k)).start()
    lax.fori_loop(this, this + 4, project(rows_a), 0)
    yown[...] = mm(attp[...], w[t])
    att2[...] = mm(attp[...], perma[...], NT).astype(bf16)
    gather_b_far()

    def add_za(j):
        drain(za.at[j], r_za.at[j])
        blk = yb.at[this + j, rows_a]
        blk[...] = (blk[...].astype(f32) + za[j].astype(f32)).astype(bf16)

    drain(zrecv, r_dz)

    share = xsum[cz].astype(f32)
    for k in range(3):
        share += zrecv[k].astype(f32)
    share = share * (adapter_scale / 8192.0)
    for c in state[1:]:
        c.wait()
    gb_s[...] = share[0:16]
    ga_s[...] = share[16:32]
    for h in range(4):
        r = slice(h * 4, h * 4 + 4)
        new_p, new_m, new_v = adam_step(ma[h], oa[h], va[h], ga_s[r, 0:64])
        nma_o[h], noa_o[h], nva_o[h] = new_p, new_m, new_v
        ga_s[r, 0:64] = new_p
    for c in range(5):
        r = slice(c * 2, c * 2 + 2)
        l = slice(c * 128, (c + 1) * 128)
        new_p, new_m, new_v = adam_step(mb[:, l], ob[:, l], vb[:, l], gb_s[r, :])
        nmb_o[:, l], nob_o[:, l], nvb_o[:, l] = new_p, new_m, new_v
        gb_s[r, :] = new_p
    mine = core * 16 + chip
    fac[mine] = jnp.concatenate([gb_s[...], ga_s[...]], axis=0).astype(bf16)

    for k in range(1, 4):
        remote(fac.at[mine], fac.at[mine], s_fz, r_fz, zpeer(k)).start()
    send_za(ynext[0])
    send_za(ynext[1])
    gather_relay(1)
    add_za(yfar)
    y_far(0)

    thr = both[:, 64:128]
    add = [mm(thr, olda[h]) for h in range(4)]
    gacc[...] = adapter_scale * jnp.concatenate(add, axis=1) + mm(cot[...], w[t], NT)

    y_relay(2)
    y_raw(2)
    mycol = pl.ds(core * 16 + cx * 4, 4)
    drain(fac.at[pl.ds(0, 3)], r_fz)
    for k in range(1, 4):
        remote(fac.at[mycol], fac.at[mycol], s_fx, r_fx, xpeer(k)).start()
    y_relay(1)
    y_raw(1)

    mycore = pl.ds(core * 16, 16)
    drain(fac.at[pl.ds(0, 12)], r_fx)
    fc = remote(fac.at[mycore], fac.at[mycore], s_fcore, r_fcore, corepeer)
    fc.start()
    fc.wait_recv()

    a_new = fac[:, 16:32, :].reshape(512, 128)
    low = mm(att2[...], a_new)[:, 0:64]
    low = jnp.concatenate([low[0:192], low[192:384]], axis=1)
    lsend[0] = low.astype(bf16)
    lz = remote(lsend.at[0], lpeer, s_lz, r_lz, zdev)
    lz.start()
    b_new = mm(gather[...], fac[:, 0:16, :].reshape(512, 128)).astype(bf16)
    b_new = jnp.concatenate([b_new[c * 64 : (c + 1) * 64] for c in range(5)], axis=1)

    lz.wait_recv()
    low += lpeer[...].astype(f32)
    lsend[1] = low.astype(bf16)
    for k in range(1, 4):
        remote(lsend.at[1], lrecv.at[3 - k], s_low, r_low, (dp, this + (y + k) % 4)).start()

    for d in range(2):
        add_za(ynext[d])
    y_relay(0)
    y_raw(0)

    y_wait(2)
    for h in range(2):
        blk = part_of(2, y, h)
        blk[...] = (blk[...].astype(f32) + y_total(2, h)).astype(bf16)
    zb = remote(yb.at[twin, rows_b], zbr, s_zb, r_zb, zdev)
    zb.start()
    send_za(y)

    for d in range(2):
        for p in range(2):
            drain(cgat.at[(other if p else this) + yprev[d], a_half(1 - d)], r_ag.at[d, 1 + p * 2 + 1 - d])
            drain(cgat.at[(other if p else this) + yfar, a_half(d)], r_ag.at[d, 6 + p])
        drain(cgat.at[other + yprev[d], gather_b], r_gz.at[3 + d])
    drain(cgat.at[twin, gather_b], r_gz.at[2])
    drain(cgat.at[other + yfar, gather_b], r_gz.at[5])

    def accumulate(k, _):
        src = jnp.where(k < 3, z, 1 - z) * 4 + (y + 1 + k) % 4
        gacc[...] += mm(cgat[src], w[src], NT)
        return 0

    lax.fori_loop(0, 7, accumulate, 0)
    grad_o[...] = gacc[...].astype(bf16)

    drain(lrecv, r_low)
    for k in range(3):
        low += lrecv[k].astype(f32)
    low = jnp.concatenate([low[:, 0:64], low[:, 64:128]], axis=0)
    hi = low.astype(bf16)
    lo = (low - hi.astype(f32)).astype(bf16)
    yown[...] += adapter_scale * (mm(hi, b_new) + mm(lo, b_new))

    drain(za.at[y], r_za.at[y])
    yown[rows_a] += za[y].astype(f32)
    y_wait(1)
    for h in range(2):
        yown[pl.ds(192 + h * half_rows, half_rows)] += y_total(1, h)
    zb.wait_recv()
    yown[rows_b] += zbr[...].astype(f32)
    y_wait(0)
    for h in range(2):
        yown[pl.ds(h * half_rows, half_rows)] += y_total(0, h)
    out_o[...] = yown[...].T.astype(bf16)

    cc.wait_send()
    fc.wait_send()
    zb.wait_send()
    lz.wait_send()
    drain(prs, s_prs)
    drain(lowf.at[pl.ds(0, 7)], s_pag)
    drain(cgat.at[0, pl.ds(64, 192)], s_gz)
    drain(cgat.at[pl.ds(0, 6), pl.ds(64, 192)], s_ag)
    drain(cgat.at[pl.ds(0, 3), gather_b], s_gb)
    drain(cgat.at[pl.ds(0, 4), gather_b], s_gbz)
    drain(xrecv, s_dx)
    drain(zrecv, s_dz)
    drain(fac.at[pl.ds(0, 3)], s_fz)
    drain(fac.at[pl.ds(0, 12)], s_fx)
    drain(za, s_za)
    for c in range(3):
        for sem in (s_p1, s_raw, s_p2):
            drain(far.at[c], sem.at[c])
    drain(lrecv, s_low)


def hand_over(*refs):
    n = (len(refs) - 1) // 2
    copies = [pltpu.make_async_copy(refs[i], refs[n + i], refs[-1].at[i]) for i in range(n)]
    for c in copies:
        c.start()
    for c in copies:
        c.wait()


def per_device(
    acts, cotangent, out_weight, old_a, old_b, master_a, master_b, moment_a, moment_b, second_a, second_b,
    key_cache, value_cache, lengths, new_query, new_key, new_value,
):
    hbm = pl.BlockSpec(memory_space=pl.ANY)
    vmem = pl.BlockSpec(memory_space=pltpu.VMEM)
    dma = pltpu.SemaphoreType.DMA
    V = pltpu.VMEM
    shp = jax.ShapeDtypeStruct
    results = pl.pallas_call(
        kernel,
        out_shape=(
            V((256, 512), bf16), V((4, 4, 64), f32), V((2, 640), f32), V((4, 4, 64), f32),
            V((2, 640), f32), V((4, 4, 64), f32), V((2, 640), f32), V((640, 384), bf16),
        ),
        in_specs=[hbm] * 17,
        out_specs=(vmem,) * 8,
        scratch_shapes=[
            V((256, 512), bf16), V((256, 640), bf16), V((8, 512, 640), bf16), V((4, 64, 128), bf16),
            V((64, 640), bf16), V((128, 48, 128), bf16), V((128, 48, 128), bf16), V((3, 128, 512), bf16),
            V((3, 128, 128), bf16), V((3, 128, 128), bf16),
            V((4, 4, 64), f32), V((2, 640), f32), V((4, 4, 64), f32), V((2, 640), f32),
            V((4, 4, 64), f32), V((2, 640), f32), V((1, 128), jnp.int32),
            V((512, 512), bf16), V((512, 320), bf16), V((320, 512), bf16), V((192, 192), bf16),
            V((16, 768), jnp.int32), V((192, 48), f32), V((128, 128), f32),
            V((8, 32, 128), f32), V((7, 32, 128), f32), V((32, 128), bf16), V((8, 32, 128), bf16),
            V((8, 256, 640), bf16), V((256, 512), f32),
            V((32, 32, 128), bf16), V((16, 32, 128), bf16), V((16, 32, 128), bf16), V((3, 4, 32, 128), bf16),
            V((4, 32, 128), bf16), V((3, 32, 128), bf16),
            V((16, 128), f32), V((16, 128), f32), V((32, 32, 128), bf16),
            V((3, 128, 512), bf16), V((384, 512), bf16), V((384, 512), bf16),
            V((8, 384, 640), bf16), V((384, 640), f32), V((4, 192, 640), bf16),
            V((3, 2, 96, 640), bf16), V((3, 2, 2, 96, 640), bf16), V((192, 640), bf16), V((2, 192, 128), bf16), V((192, 128), bf16),
            V((3, 192, 128), bf16),
            dma((24,)), dma, dma, dma, dma, dma, dma((2, 8)), dma, dma((6,)), dma, dma, dma, dma, dma, dma, dma, dma, dma, dma,
            dma, dma, dma, dma, dma, dma((4,)), dma((3,)), dma((3, 2)), dma((3,)), dma((3, 2)), dma((3,)), dma((3, 2)),
            dma, dma, dma, dma, dma, dma,
        ],
        compiler_params=pltpu.CompilerParams(
            collective_id=0, has_side_effects=True, vmem_limit_bytes=56 << 20
        ),
        cost_estimate=pl.CostEstimate(flops=4 << 30, bytes_accessed=12 << 20, transcendentals=1 << 20),
        name="update_and_decode",
    )(
        acts, cotangent, out_weight, old_a.swapaxes(1, 2), old_b,
        master_a, master_b, moment_a, moment_b, second_a, second_b,
        key_cache.reshape(128, 48, 128), value_cache.reshape(128, 48, 128), lengths.reshape(1, 128),
        new_query.swapaxes(0, 1), new_key.swapaxes(0, 1), new_value.swapaxes(0, 1),
    )
    return pl.pallas_call(
        hand_over,
        out_shape=tuple(shp(r.shape, r.dtype) for r in results),
        in_specs=[vmem] * 8,
        out_specs=(hbm,) * 8,
        scratch_shapes=[dma((8,))],
        cost_estimate=pl.CostEstimate(flops=0, bytes_accessed=2 << 20, transcendentals=0),
        name="hand_over",
    )(*(pltpu.with_memory_space_constraint(r, pltpu.VMEM) for r in results))


def solution(mesh):
    return jax.shard_map(
        per_device,
        mesh=mesh,
        in_specs=(
            P("dp", "tensor"),
            P("dp", "tensor"),
            P("tensor", None),
            P("tensor", None, None),
            P(),
            P("tensor", "dp", None),
            P("dp", "tensor"),
            P("tensor", "dp", None),
            P("dp", "tensor"),
            P("tensor", "dp", None),
            P("dp", "tensor"),
            P("dp", "tensor", None, None),
            P("dp", "tensor", None, None),
            P("dp"),
            P("dp", None, "tensor"),
            P("dp", None, "tensor"),
            P("dp", None, "tensor"),
        ),
        out_specs=(
            P("dp", "tensor"),
            P("tensor", "dp", None),
            P("dp", "tensor"),
            P("tensor", "dp", None),
            P("dp", "tensor"),
            P("tensor", "dp", None),
            P("dp", "tensor"),
            P("tensor", "dp"),
        ),
        check_vma=False,
    )
```

```python
import functools

import jax
import jax.numpy as jnp
from jax import lax
from jax.experimental import pallas as pl
from jax.experimental.pallas import tpu as pltpu
from jax.sharding import PartitionSpec as P

adapter_scale = 2.0
beta_one = 0.9
beta_two = 0.999
learn_rate = 0.01
decay_rate = 0.01
corr_one = 1.0 - 0.9**10
corr_two = 1.0 - 0.999**10
MESH = pl.DeviceIdType.MESH
f32 = jnp.float32
bf16 = jnp.bfloat16
NT = (((1,), (1,)), ((), ()))
NN = (((1,), (0,)), ((), ()))


def mm(a, b, dims=NN):
    return lax.dot_general(a, b, dims, preferred_element_type=f32)


def iota(shape, dim):
    return lax.broadcasted_iota(jnp.int32, shape, dim)


def onehot(hit):
    return jnp.where(hit, 1.0, 0.0).astype(f32).astype(bf16)


def adam_step(master, moment, second, grad):
    moment_new = beta_one * moment + (1.0 - beta_one) * grad
    second_new = beta_two * second + (1.0 - beta_two) * grad * grad
    update = moment_new / corr_one / (jnp.sqrt(second_new / corr_two) + 1e-08)
    return (master - learn_rate * (update + decay_rate * master), moment_new, second_new)


def kernel(
    acts_h, cot_h, w_h, olda_h, oldb_h,
    ma_h, mb_h, oa_h, ob_h, va_h, vb_h,
    key_h, val_h, len_h, q_h, nk_h, nv_h,
    grad_o, nma_o, nmb_o, noa_o, nob_o, nva_o, nvb_o, out_o,
    acts, cot, w, olda, oldb, keys, vals, q, nk, nv,
    ma, mb, oa, ob, va, vb, len_ref,
    perma, spread, gather, permr, slotm, freshb, lencol,
    part, prs, lows, lowf, cgat, gacc,
    gst, gpeer, hsum, xrecv, xsum, zrecv, ga_s, gb_s, fac,
    att, attp, att2, yb, yown, za, far, fin, zbr, lsend, lpeer, lrecv,
    lsem, s_prs, r_prs, s_pag, r_pag, s_ag, r_ag, s_gz, r_gz, s_gb, s_gbz, s_core, r_core, s_dx, r_dx, s_dz, r_dz,
    s_fz, r_fz, s_fx, r_fx, s_fcore, r_fcore, s_za, r_za, s_p1, r_p1, s_raw, r_raw, s_p2, r_p2, s_zb, r_zb, s_lz, r_lz, s_low, r_low,
):
    dp = lax.axis_index("dp")
    t = lax.axis_index("tensor")
    chip = dp // 2
    core = dp % 2
    z = t // 4
    y = t % 4

    def tpeer(k):
        return (dp, (t + k) % 8)

    cx, cz = chip // 4, chip % 4

    def xpeer(k):
        return ((((cx + k) % 4) * 4 + cz) * 2 + core, t)

    def zpeer(k):
        return ((cx * 4 + (cz + k) % 4) * 2 + core, t)

    corepeer = (chip * 2 + 1 - core, t)
    twin = (1 - z) * 4 + y
    zdev = (dp, twin)
    ynext = ((y + 1) % 4, (y + 3) % 4)
    yfar = (y + 2) % 4
    ydev = tuple((dp, z * 4 + n) for n in ynext)
    yprev = (ynext[1], ynext[0])

    def remote(src, dst, ssem, rsem, dev):
        return pltpu.make_async_remote_copy(
            src_ref=src, dst_ref=dst, send_sem=ssem, recv_sem=rsem, device_id=dev, device_id_type=MESH
        )

    def drain(ref, sem):
        pltpu.make_async_copy(ref, ref, sem).wait()

    loads = [
        pltpu.make_async_copy(acts_h, acts, lsem.at[0]),
        pltpu.make_async_copy(cot_h, cot, lsem.at[1]),
        pltpu.make_async_copy(olda_h, olda, lsem.at[2]),
        pltpu.make_async_copy(oldb_h.at[:, pl.ds(pl.multiple_of(t * 640, 128), 640)], oldb, lsem.at[3]),
        pltpu.make_async_copy(q_h, q, lsem.at[4]),
        pltpu.make_async_copy(key_h, keys, lsem.at[5]),
        pltpu.make_async_copy(nk_h, nk, lsem.at[6]),
        pltpu.make_async_copy(val_h, vals, lsem.at[7]),
        pltpu.make_async_copy(nv_h, nv, lsem.at[8]),
    ]
    for j in range(8):
        loads.append(pltpu.make_async_copy(w_h.at[:, pl.ds(j * 640, 640)], w.at[j], lsem.at[9 + j]))
    small = ((len_h, len_ref), (ma_h, ma), (mb_h, mb), (oa_h, oa), (ob_h, ob), (va_h, va), (vb_h, vb))
    state = [pltpu.make_async_copy(a, b, lsem.at[17 + i]) for i, (a, b) in enumerate(small)]
    for c in loads + state:
        c.start()

    bar = pltpu.get_barrier_semaphore()

    def sig_t(k, _):
        pl.semaphore_signal(bar, inc=1, device_id=tpeer(k), device_id_type=MESH)
        return 0

    def sig_c(k, _):
        pl.semaphore_signal(bar, inc=1, device_id=xpeer(k), device_id_type=MESH)
        pl.semaphore_signal(bar, inc=1, device_id=zpeer(k), device_id_type=MESH)
        return 0

    lax.fori_loop(1, 8, sig_t, 0)
    lax.fori_loop(1, 4, sig_c, 0)
    pl.semaphore_signal(bar, inc=1, device_id=corepeer, device_id_type=MESH)

    pl.semaphore_wait(bar, 14)

    gather_b = pl.ds(0, 96)

    def b_half(h):
        return pl.ds(h * 48, 48)

    def a_half(h):
        return pl.ds(96 + h * 80, 80)

    def gather_own_z(h):
        remote(cot.at[a_half(h)], cgat.at[t, a_half(h)], s_gz, r_gz.at[h], zdev).start()

    def gather_own_y(h):
        for d in range(2):
            remote(cot.at[a_half(h)], cgat.at[t, a_half(h)], s_ag, r_ag.at[d, 1 + h], ydev[d]).start()

    def gather_twin(h):
        blk = cgat.at[twin, a_half(h)]
        drain(blk, r_gz.at[h])
        for d in range(2):
            remote(blk, blk, s_ag, r_ag.at[d, 3 + h], ydev[d]).start()

    def gather_relay(which):
        for d in range(2):
            blk = cgat.at[(z if which == 0 else 1 - z) * 4 + yprev[d], a_half(d)]
            drain(blk, r_ag.at[d, 1 + which * 2 + d])
            remote(blk, blk, s_ag, r_ag.at[d, 6 + which], ydev[d]).start()

    def gather_b_own():
        for d in range(2):
            remote(cot.at[gather_b], cgat.at[t, gather_b], s_gb, r_ag.at[d, 0], ydev[d]).start()

    def gather_b_relay():
        for d in range(2):
            drain(cgat.at[z * 4 + yprev[d], gather_b], r_ag.at[d, 0])
            blk = cgat.at[z * 4 + yprev[d], b_half(d)]
            remote(blk, blk, s_gb, r_ag.at[d, 5], ydev[d]).start()

    def gather_b_twin():
        remote(cot.at[gather_b], cgat.at[t, gather_b], s_gbz, r_gz.at[2], zdev).start()

    def gather_b_next():
        for d in range(2):
            blk = cgat.at[z * 4 + yprev[d], gather_b]
            remote(blk, blk, s_gbz, r_gz.at[3 + d], zdev).start()

    def gather_b_far():
        for d in range(2):
            drain(cgat.at[z * 4 + yfar, b_half(d)], r_ag.at[d, 5])
        blk = cgat.at[z * 4 + yfar, gather_b]
        remote(blk, blk, s_gbz, r_gz.at[5], zdev).start()

    loads[1].wait()
    gather_b_own()
    gather_own_z(0)

    for c in (loads[0], loads[2], loads[3]):
        c.wait()
    low_p = mm(acts[:, 0:128], olda[0], NT)
    for h in range(1, 4):
        low_p += mm(acts[:, h * 128 : (h + 1) * 128], olda[h], NT)
    thr_p = mm(cot[...], oldb[...], NT)
    part[...] = jnp.concatenate([low_p, thr_p], axis=1).astype(bf16).reshape(8, 32, 128)
    def send_part(k, _):
        remote(part.at[(t + k) % 8], prs.at[7 - k], s_prs, r_prs, tpeer(k)).start()
        return 0

    lax.fori_loop(1, 8, send_part, 0)

    gather_own_y(0)
    gather_b_twin()

    prow, pcol = iota((512, 512), 0), iota((512, 512), 1)
    blk = prow >> 4
    perma[...] = onehot(
        pcol == (((prow >> 2) & 3) << 7) + (((blk & 15) * 2 + (blk >> 4)) << 2) + (prow & 3)
    )
    erow, ecol = iota((512, 320), 0), iota((512, 320), 1)
    blk = erow >> 4
    idx = erow & 15
    spread[...] = onehot(
        (idx < 10) & (ecol == ((idx >> 1) << 6) + ((blk & 15) * 2 + (blk >> 4)) * 2 + (idx & 1))
    )
    erow, ecol = iota((320, 512), 1), iota((320, 512), 0)
    blk = erow >> 4
    idx = erow & 15
    gather[...] = onehot(
        (idx < 10) & (ecol == ((idx >> 1) << 6) + ((blk & 15) * 2 + (blk >> 4)) * 2 + (idx & 1))
    )
    rj, rk = iota((192, 192), 0), iota((192, 192), 1)
    permr[...] = onehot((rj - 3 * (rk & 63)) == (rk >> 6))
    slot = iota((16, 768), 1) - 48 * iota((16, 768), 0)
    slotm[...] = jnp.where((slot >= 0) & (slot < 48), slot, 1000)
    fr, fc = iota((192, 48), 0), iota((192, 48), 1)
    freshb[...] = jnp.where(((fr & 15) == (fc & 15)) & ((fc >> 4) <= (fr >> 6)), 0.0, -1e30).astype(f32)
    state[0].wait()
    diag = iota((128, 128), 0) == iota((128, 128), 1)
    lencol[...] = jnp.broadcast_to(
        jnp.sum(jnp.where(diag, len_ref[...].astype(f32), 0.0), axis=1, keepdims=True), (128, 128)
    )

    scale = f32(1.0) / jnp.sqrt(f32(128.0))

    def attend(g, _):
        rows = pl.ds(pl.multiple_of(g * 16, 16), 16)
        qg = jnp.concatenate(
            [q[s, rows, h * 128 : (h + 1) * 128] for s in range(3) for h in range(4)], axis=0
        )
        kg = keys[rows].reshape(768, 128)
        vg = vals[rows].reshape(768, 128)
        nkg = jnp.concatenate([nk[s, rows, :] for s in range(3)], axis=0)
        nvg = jnp.concatenate([nv[s, rows, :] for s in range(3)], axis=0)
        bias = jnp.where(slotm[...].astype(f32) < lencol[rows, 0:1], 0.0, -1e30).astype(f32)
        s1 = (mm(qg, kg, NT) * scale).reshape(12, 16, 768) + bias[None]
        s1 = s1.reshape(192, 768)
        s2 = mm(qg, nkg, NT) * scale + freshb[...]
        top = jnp.maximum(jnp.max(s1, axis=1, keepdims=True), jnp.max(s2, axis=1, keepdims=True))
        e1 = jnp.exp(s1 - top)
        e2 = jnp.exp(s2 - top)
        inv = 1.0 / (jnp.sum(e1, axis=1, keepdims=True) + jnp.sum(e2, axis=1, keepdims=True))
        o = mm((e1 * inv).astype(bf16), vg) + mm((e2 * inv).astype(bf16), nvg)
        o = o.astype(bf16)
        for s in range(3):
            for h in range(4):
                i = (s * 4 + h) * 16
                att[s, rows, h * 128 : (h + 1) * 128] = o[i : i + 16]
        return 0

    rows_a = pl.ds(0, 192)
    rows_b = pl.ds(192, 192)

    def order_rows(i):
        block = att[:, i * 64 : (i + 1) * 64, :].reshape(192, 512)
        attp[pl.ds(i * 192, 192)] = mm(permr[...], block).astype(bf16)

    def project(rows):
        def one(j, _):
            yb[j, rows] = mm(attp[rows], w[j]).astype(bf16)
            return 0

        return one

    this, other = z * 4, (1 - z) * 4

    def send_za(j, h):
        part_h = pl.ds(h * 96, 96)
        remote(yb.at[other + j, part_h], za.at[j, part_h], s_za, r_za.at[j], zdev).start()

    half_rows = 96
    classes = ((0, z), (192, z), (192, 1 - z))

    def part_of(c, owner, h):
        r0, plane = classes[c]
        return yb.at[plane * 4 + owner, pl.ds(r0 + h * half_rows, half_rows)]

    def y_far(c):
        for d in range(2):
            remote(part_of(c, yfar, d), far.at[c, d], s_p1.at[c], r_p1.at[c, d], ydev[d]).start()

    def y_raw(c):
        for d in range(2):
            remote(
                part_of(c, ynext[d], 1 - d), fin.at[c, d, 1 - d], s_raw.at[c], r_raw.at[c, d], ydev[d]
            ).start()

    def y_relay(c):
        for d in range(2):
            drain(far.at[c, d], r_p1.at[c, d])
            blk = part_of(c, ynext[d], d)
            blk[...] = (blk[...].astype(f32) + far[c, d].astype(f32)).astype(bf16)
            remote(blk, fin.at[c, d, d], s_p2.at[c], r_p2.at[c, d], ydev[d]).start()

    def y_total(c, h):
        return fin[c, 0, h].astype(f32) + fin[c, 1, h].astype(f32)

    def y_wait(c):
        for d in range(2):
            drain(fin.at[c, d, 1 - d], r_raw.at[c, d])
            drain(fin.at[c, d, d], r_p2.at[c, d])

    for c in loads[4:9]:
        c.wait()
    lax.fori_loop(0, 4, attend, 0)
    order_rows(0)

    gather_own_z(1)
    gather_own_y(1)
    drain(prs, r_prs)
    tot = part[t].astype(f32)
    for k in range(7):
        tot += prs[k].astype(f32)
    lows[...] = tot.astype(bf16)
    lowf[t] = tot.astype(bf16)

    def send_low(k, _):
        remote(lows, lowf.at[t], s_pag, r_pag, tpeer(k)).start()
        return 0

    lax.fori_loop(1, 8, send_low, 0)
    for c in loads[9:]:
        c.wait()
    lax.fori_loop(other, other + 4, project(rows_a), 0)
    gather_b_relay()
    gather_twin(0)
    gather_b_next()
    lax.fori_loop(4, 6, attend, 0)

    drain(lowf.at[pl.ds(0, 7)], r_pag)

    both = lowf[...].reshape(256, 128)
    both_t = both.astype(f32).T.astype(bf16)
    ga_t = mm(both_t[64:128], acts[...]).astype(bf16)
    gb = mm(both_t[0:64], cot[...]).astype(bf16)
    ga = mm(perma[...], ga_t, NT)
    gb = jnp.concatenate([gb[:, c * 128 : (c + 1) * 128] for c in range(5)], axis=0)
    gb = mm(spread[...], gb)
    gst[:, 0:16, :] = gb.astype(bf16).reshape(32, 16, 128)
    gst[:, 16:32, :] = jnp.concatenate([ga, jnp.zeros_like(ga)], axis=1).astype(bf16).reshape(32, 16, 128)
    cc = remote(gst.at[pl.ds((1 - core) * 16, 16)], gpeer, s_core, r_core, corepeer)
    cc.start()

    lax.fori_loop(6, 8, attend, 0)
    gather_twin(1)
    gather_relay(0)
    cc.wait_recv()
    hsum[...] = (gst[pl.ds(core * 16, 16)].astype(f32) + gpeer[...].astype(f32)).astype(bf16)

    for k in range(1, 4):
        remote(hsum.at[pl.ds((cx + k) % 4 * 4, 4)], xrecv.at[3 - k], s_dx, r_dx, xpeer(k)).start()
    send_za(yfar, 0)
    send_za(yfar, 1)
    order_rows(1)
    lax.fori_loop(other, other + 4, project(rows_b), 0)
    y_far(2)
    lax.fori_loop(this, this + 4, project(rows_b), 0)
    y_far(1)
    drain(xrecv, r_dx)
    xtot = hsum[pl.ds(cx * 4, 4)].astype(f32)
    for k in range(3):
        xtot += xrecv[k].astype(f32)
    xsum[...] = xtot.astype(bf16)
    for k in range(1, 4):
        remote(xsum.at[(cz + k) % 4], zrecv.at[3 - k], s_dz, r_dz, zpeer(k)).start()
    gather_b_far()
    lax.fori_loop(this, this + 4, project(rows_a), 0)
    yown[...] = mm(attp[...], w[t])
    att2[...] = mm(attp[...], perma[...], NT).astype(bf16)
    def add_za(j):
        drain(za.at[j], r_za.at[j])
        blk = yb.at[this + j, rows_a]
        blk[...] = (blk[...].astype(f32) + za[j].astype(f32)).astype(bf16)

    gather_relay(1)
    add_za(yfar)
    y_far(0)
    y_raw(2)
    y_raw(1)
    send_za(ynext[0], 0)

    drain(zrecv, r_dz)

    share = xsum[cz].astype(f32)
    for k in range(3):
        share += zrecv[k].astype(f32)
    share = share * (adapter_scale / 8192.0)
    for c in state[1:]:
        c.wait()
    gb_s[...] = share[0:16]
    ga_s[...] = share[16:32]
    for h in range(4):
        r = slice(h * 4, h * 4 + 4)
        new_p, new_m, new_v = adam_step(ma[h], oa[h], va[h], ga_s[r, 0:64])
        nma_o[h], noa_o[h], nva_o[h] = new_p, new_m, new_v
        ga_s[r, 0:64] = new_p
    for c in range(5):
        r = slice(c * 2, c * 2 + 2)
        l = slice(c * 128, (c + 1) * 128)
        new_p, new_m, new_v = adam_step(mb[:, l], ob[:, l], vb[:, l], gb_s[r, :])
        nmb_o[:, l], nob_o[:, l], nvb_o[:, l] = new_p, new_m, new_v
        gb_s[r, :] = new_p
    mine = core * 16 + chip
    fac[mine] = jnp.concatenate([gb_s[...], ga_s[...]], axis=0).astype(bf16)

    for k in range(1, 4):
        remote(fac.at[mine], fac.at[mine], s_fz, r_fz, zpeer(k)).start()
    send_za(ynext[0], 1)
    for h in range(2):
        send_za(ynext[1], h)
    for h in range(2):
        send_za(y, h)

    thr = both[:, 64:128]
    add = [mm(thr, olda[h]) for h in range(4)]
    gacc[...] = adapter_scale * jnp.concatenate(add, axis=1) + mm(cot[...], w[t], NT)

    y_relay(2)
    y_relay(1)
    mycol = pl.ds(core * 16 + cx * 4, 4)
    drain(fac.at[pl.ds(0, 3)], r_fz)
    for k in range(1, 4):
        remote(fac.at[mycol], fac.at[mycol], s_fx, r_fx, xpeer(k)).start()

    mycore = pl.ds(core * 16, 16)
    drain(fac.at[pl.ds(0, 12)], r_fx)
    fc = remote(fac.at[mycore], fac.at[mycore], s_fcore, r_fcore, corepeer)
    fc.start()
    fc.wait_recv()

    a_new = fac[:, 16:32, :].reshape(512, 128)
    low = mm(att2[...], a_new)[:, 0:64]
    low = jnp.concatenate([low[0:192], low[192:384]], axis=1)
    lsend[0] = low.astype(bf16)
    lz = remote(lsend.at[0], lpeer, s_lz, r_lz, zdev)
    lz.start()
    b_new = mm(gather[...], fac[:, 0:16, :].reshape(512, 128)).astype(bf16)
    b_new = jnp.concatenate([b_new[c * 64 : (c + 1) * 64] for c in range(5)], axis=1)

    for d in range(2):
        add_za(ynext[d])
    y_relay(0)
    y_raw(0)

    y_wait(2)
    for h in range(2):
        blk = part_of(2, y, h)
        blk[...] = (blk[...].astype(f32) + y_total(2, h)).astype(bf16)
    zb = remote(yb.at[twin, rows_b], zbr, s_zb, r_zb, zdev)
    zb.start()

    lz.wait_recv()
    low += lpeer[...].astype(f32)
    lsend[1] = low.astype(bf16)
    for k in range(1, 4):
        remote(lsend.at[1], lrecv.at[3 - k], s_low, r_low, (dp, this + (y + k) % 4)).start()

    for d in range(2):
        for p in range(2):
            drain(cgat.at[(other if p else this) + yprev[d], a_half(1 - d)], r_ag.at[d, 1 + p * 2 + 1 - d])
            drain(cgat.at[(other if p else this) + yfar, a_half(d)], r_ag.at[d, 6 + p])
        drain(cgat.at[other + yprev[d], gather_b], r_gz.at[3 + d])
    drain(cgat.at[twin, gather_b], r_gz.at[2])
    drain(cgat.at[other + yfar, gather_b], r_gz.at[5])

    def accumulate(k, _):
        src = jnp.where(k < 3, z, 1 - z) * 4 + (y + 1 + k) % 4
        gacc[...] += mm(cgat[src], w[src], NT)
        return 0

    lax.fori_loop(0, 7, accumulate, 0)
    grad_o[...] = gacc[...].astype(bf16)

    drain(lrecv, r_low)
    for k in range(3):
        low += lrecv[k].astype(f32)
    low = jnp.concatenate([low[:, 0:64], low[:, 64:128]], axis=0)
    hi = low.astype(bf16)
    lo = (low - hi.astype(f32)).astype(bf16)
    yown[...] += adapter_scale * (mm(hi, b_new) + mm(lo, b_new))

    drain(za.at[y], r_za.at[y])
    yown[rows_a] += za[y].astype(f32)
    y_wait(1)
    for h in range(2):
        yown[pl.ds(192 + h * half_rows, half_rows)] += y_total(1, h)
    zb.wait_recv()
    yown[rows_b] += zbr[...].astype(f32)
    y_wait(0)
    for h in range(2):
        yown[pl.ds(h * half_rows, half_rows)] += y_total(0, h)
    out_o[...] = yown[...].T.astype(bf16)

    cc.wait_send()
    fc.wait_send()
    zb.wait_send()
    lz.wait_send()
    drain(prs, s_prs)
    drain(lowf.at[pl.ds(0, 7)], s_pag)
    drain(cgat.at[0, pl.ds(96, 160)], s_gz)
    drain(cgat.at[pl.ds(0, 6), pl.ds(96, 160)], s_ag)
    drain(cgat.at[pl.ds(0, 3), gather_b], s_gb)
    drain(cgat.at[pl.ds(0, 4), gather_b], s_gbz)
    drain(xrecv, s_dx)
    drain(zrecv, s_dz)
    drain(fac.at[pl.ds(0, 3)], s_fz)
    drain(fac.at[pl.ds(0, 12)], s_fx)
    drain(za, s_za)
    for c in range(3):
        for sem in (s_p1, s_raw, s_p2):
            drain(far.at[c], sem.at[c])
    drain(lrecv, s_low)


def hand_over(*refs):
    n = (len(refs) - 1) // 2
    copies = [pltpu.make_async_copy(refs[i], refs[n + i], refs[-1].at[i]) for i in range(n)]
    for c in copies:
        c.start()
    for c in copies:
        c.wait()


def per_device(
    acts, cotangent, out_weight, old_a, old_b, master_a, master_b, moment_a, moment_b, second_a, second_b,
    key_cache, value_cache, lengths, new_query, new_key, new_value,
):
    hbm = pl.BlockSpec(memory_space=pl.ANY)
    vmem = pl.BlockSpec(memory_space=pltpu.VMEM)
    dma = pltpu.SemaphoreType.DMA
    V = pltpu.VMEM
    shp = jax.ShapeDtypeStruct
    results = pl.pallas_call(
        kernel,
        out_shape=(
            V((256, 512), bf16), V((4, 4, 64), f32), V((2, 640), f32), V((4, 4, 64), f32),
            V((2, 640), f32), V((4, 4, 64), f32), V((2, 640), f32), V((640, 384), bf16),
        ),
        in_specs=[hbm] * 17,
        out_specs=(vmem,) * 8,
        scratch_shapes=[
            V((256, 512), bf16), V((256, 640), bf16), V((8, 512, 640), bf16), V((4, 64, 128), bf16),
            V((64, 640), bf16), V((128, 48, 128), bf16), V((128, 48, 128), bf16), V((3, 128, 512), bf16),
            V((3, 128, 128), bf16), V((3, 128, 128), bf16),
            V((4, 4, 64), f32), V((2, 640), f32), V((4, 4, 64), f32), V((2, 640), f32),
            V((4, 4, 64), f32), V((2, 640), f32), V((1, 128), jnp.int32),
            V((512, 512), bf16), V((512, 320), bf16), V((320, 512), bf16), V((192, 192), bf16),
            V((16, 768), jnp.int32), V((192, 48), f32), V((128, 128), f32),
            V((8, 32, 128), bf16), V((7, 32, 128), bf16), V((32, 128), bf16), V((8, 32, 128), bf16),
            V((8, 256, 640), bf16), V((256, 512), f32),
            V((32, 32, 128), bf16), V((16, 32, 128), bf16), V((16, 32, 128), bf16), V((3, 4, 32, 128), bf16),
            V((4, 32, 128), bf16), V((3, 32, 128), bf16),
            V((16, 128), f32), V((16, 128), f32), V((32, 32, 128), bf16),
            V((3, 128, 512), bf16), V((384, 512), bf16), V((384, 512), bf16),
            V((8, 384, 640), bf16), V((384, 640), f32), V((4, 192, 640), bf16),
            V((3, 2, 96, 640), bf16), V((3, 2, 2, 96, 640), bf16), V((192, 640), bf16), V((2, 192, 128), bf16), V((192, 128), bf16),
            V((3, 192, 128), bf16),
            dma((24,)), dma, dma, dma, dma, dma, dma((2, 8)), dma, dma((6,)), dma, dma, dma, dma, dma, dma, dma, dma, dma, dma,
            dma, dma, dma, dma, dma, dma((4,)), dma((3,)), dma((3, 2)), dma((3,)), dma((3, 2)), dma((3,)), dma((3, 2)),
            dma, dma, dma, dma, dma, dma,
        ],
        compiler_params=pltpu.CompilerParams(
            collective_id=0, has_side_effects=True, vmem_limit_bytes=56 << 20
        ),
        cost_estimate=pl.CostEstimate(flops=4 << 30, bytes_accessed=12 << 20, transcendentals=1 << 20),
        name="update_and_decode",
    )(
        acts, cotangent, out_weight, old_a.swapaxes(1, 2), old_b,
        master_a, master_b, moment_a, moment_b, second_a, second_b,
        key_cache.reshape(128, 48, 128), value_cache.reshape(128, 48, 128), lengths.reshape(1, 128),
        new_query.swapaxes(0, 1), new_key.swapaxes(0, 1), new_value.swapaxes(0, 1),
    )
    return pl.pallas_call(
        hand_over,
        out_shape=tuple(shp(r.shape, r.dtype) for r in results),
        in_specs=[vmem] * 8,
        out_specs=(hbm,) * 8,
        scratch_shapes=[dma((8,))],
        cost_estimate=pl.CostEstimate(flops=0, bytes_accessed=2 << 20, transcendentals=0),
        name="hand_over",
    )(*(pltpu.with_memory_space_constraint(r, pltpu.VMEM) for r in results))


def solution(mesh):
    return jax.shard_map(
        per_device,
        mesh=mesh,
        in_specs=(
            P("dp", "tensor"),
            P("dp", "tensor"),
            P("tensor", None),
            P("tensor", None, None),
            P(),
            P("tensor", "dp", None),
            P("dp", "tensor"),
            P("tensor", "dp", None),
            P("dp", "tensor"),
            P("tensor", "dp", None),
            P("dp", "tensor"),
            P("dp", "tensor", None, None),
            P("dp", "tensor", None, None),
            P("dp"),
            P("dp", None, "tensor"),
            P("dp", None, "tensor"),
            P("dp", None, "tensor"),
        ),
        out_specs=(
            P("dp", "tensor"),
            P("tensor", "dp", None),
            P("dp", "tensor"),
            P("tensor", "dp", None),
            P("dp", "tensor"),
            P("tensor", "dp", None),
            P("dp", "tensor"),
            P("tensor", "dp"),
        ),
        check_vma=False,
    )
```

```python
import functools

import jax
import jax.numpy as jnp
from jax import lax
from jax.experimental import pallas as pl
from jax.experimental.pallas import tpu as pltpu
from jax.sharding import PartitionSpec as P

adapter_scale = 2.0
beta_one = 0.9
beta_two = 0.999
learn_rate = 0.01
decay_rate = 0.01
corr_one = 1.0 - 0.9**10
corr_two = 1.0 - 0.999**10
MESH = pl.DeviceIdType.MESH
f32 = jnp.float32
bf16 = jnp.bfloat16
NT = (((1,), (1,)), ((), ()))
NN = (((1,), (0,)), ((), ()))


def mm(a, b, dims=NN):
    return lax.dot_general(a, b, dims, preferred_element_type=f32)


def iota(shape, dim):
    return lax.broadcasted_iota(jnp.int32, shape, dim)


def onehot(hit):
    return jnp.where(hit, 1.0, 0.0).astype(f32).astype(bf16)


def adam_step(master, moment, second, grad):
    moment_new = beta_one * moment + (1.0 - beta_one) * grad
    second_new = beta_two * second + (1.0 - beta_two) * grad * grad
    update = moment_new / corr_one / (jnp.sqrt(second_new / corr_two) + 1e-08)
    return (master - learn_rate * (update + decay_rate * master), moment_new, second_new)


def kernel(
    acts_h, cot_h, w_h, olda_h, oldb_h,
    ma_h, mb_h, oa_h, ob_h, va_h, vb_h,
    key_h, val_h, len_h, q_h, nk_h, nv_h,
    grad_o, nma_o, nmb_o, noa_o, nob_o, nva_o, nvb_o, out_o,
    acts, cot, w, olda, oldb, keys, vals, q, nk, nv,
    ma, mb, oa, ob, va, vb, len_ref,
    perma, spread, gather, permr, slotm, freshb, lencol,
    part, prs, lows, lowf, cgat, gacc,
    gst, gpeer, hsum, xrecv, xsum, zrecv, ga_s, gb_s, fac,
    att, attp, att2, yb, yown, za, far, fin, zbr, lsend, lpeer, lrecv,
    lsem, s_prs, r_prs, s_pag, r_pag, s_ag, r_ag, s_gz, r_gz, s_gb, s_gbz, s_core, r_core, s_dx, r_dx, s_dz, r_dz,
    s_fz, r_fz, s_fx, r_fx, s_fcore, r_fcore, s_za, r_za, s_p1, r_p1, s_raw, r_raw, s_p2, r_p2, s_zb, r_zb, s_lz, r_lz, s_low, r_low,
):
    dp = lax.axis_index("dp")
    t = lax.axis_index("tensor")
    chip = dp // 2
    core = dp % 2
    z = t // 4
    y = t % 4

    def tpeer(k):
        return (dp, (t + k) % 8)

    cx, cz = chip // 4, chip % 4

    def xpeer(k):
        return ((((cx + k) % 4) * 4 + cz) * 2 + core, t)

    def zpeer(k):
        return ((cx * 4 + (cz + k) % 4) * 2 + core, t)

    corepeer = (chip * 2 + 1 - core, t)
    twin = (1 - z) * 4 + y
    zdev = (dp, twin)
    ynext = ((y + 1) % 4, (y + 3) % 4)
    yfar = (y + 2) % 4
    ydev = tuple((dp, z * 4 + n) for n in ynext)
    yprev = (ynext[1], ynext[0])

    def remote(src, dst, ssem, rsem, dev):
        return pltpu.make_async_remote_copy(
            src_ref=src, dst_ref=dst, send_sem=ssem, recv_sem=rsem, device_id=dev, device_id_type=MESH
        )

    def drain(ref, sem):
        pltpu.make_async_copy(ref, ref, sem).wait()

    loads = [
        pltpu.make_async_copy(acts_h, acts, lsem.at[0]),
        pltpu.make_async_copy(cot_h, cot, lsem.at[1]),
        pltpu.make_async_copy(olda_h, olda, lsem.at[2]),
        pltpu.make_async_copy(oldb_h.at[:, pl.ds(pl.multiple_of(t * 640, 128), 640)], oldb, lsem.at[3]),
        pltpu.make_async_copy(q_h, q, lsem.at[4]),
        pltpu.make_async_copy(key_h, keys, lsem.at[5]),
        pltpu.make_async_copy(nk_h, nk, lsem.at[6]),
        pltpu.make_async_copy(val_h, vals, lsem.at[7]),
        pltpu.make_async_copy(nv_h, nv, lsem.at[8]),
    ]
    for j in range(8):
        loads.append(pltpu.make_async_copy(w_h.at[:, pl.ds(j * 640, 640)], w.at[j], lsem.at[9 + j]))
    small = ((len_h, len_ref), (ma_h, ma), (mb_h, mb), (oa_h, oa), (ob_h, ob), (va_h, va), (vb_h, vb))
    state = [pltpu.make_async_copy(a, b, lsem.at[17 + i]) for i, (a, b) in enumerate(small)]
    for c in loads + state:
        c.start()

    bar = pltpu.get_barrier_semaphore()

    def sig_t(k, _):
        pl.semaphore_signal(bar, inc=1, device_id=tpeer(k), device_id_type=MESH)
        return 0

    def sig_c(k, _):
        pl.semaphore_signal(bar, inc=1, device_id=xpeer(k), device_id_type=MESH)
        pl.semaphore_signal(bar, inc=1, device_id=zpeer(k), device_id_type=MESH)
        return 0

    lax.fori_loop(1, 8, sig_t, 0)
    lax.fori_loop(1, 4, sig_c, 0)
    pl.semaphore_signal(bar, inc=1, device_id=corepeer, device_id_type=MESH)

    pl.semaphore_wait(bar, 14)

    gather_b = pl.ds(0, 96)

    def b_half(h):
        return pl.ds(h * 48, 48)

    def a_half(h):
        return pl.ds(96 + h * 80, 80)

    def gather_own_z(h):
        remote(cot.at[a_half(h)], cgat.at[t, a_half(h)], s_gz, r_gz.at[h], zdev).start()

    def gather_own_y(h):
        for d in range(2):
            remote(cot.at[a_half(h)], cgat.at[t, a_half(h)], s_ag, r_ag.at[d, 1 + h], ydev[d]).start()

    def gather_twin(h):
        blk = cgat.at[twin, a_half(h)]
        drain(blk, r_gz.at[h])
        for d in range(2):
            remote(blk, blk, s_ag, r_ag.at[d, 3 + h], ydev[d]).start()

    def gather_relay(which):
        for d in range(2):
            blk = cgat.at[(z if which == 0 else 1 - z) * 4 + yprev[d], a_half(d)]
            drain(blk, r_ag.at[d, 1 + which * 2 + d])
            remote(blk, blk, s_ag, r_ag.at[d, 6 + which], ydev[d]).start()

    def gather_b_own():
        for d in range(2):
            remote(cot.at[gather_b], cgat.at[t, gather_b], s_gb, r_ag.at[d, 0], ydev[d]).start()

    def gather_b_relay():
        for d in range(2):
            drain(cgat.at[z * 4 + yprev[d], gather_b], r_ag.at[d, 0])
            blk = cgat.at[z * 4 + yprev[d], b_half(d)]
            remote(blk, blk, s_gb, r_ag.at[d, 5], ydev[d]).start()

    def gather_b_twin():
        remote(cot.at[gather_b], cgat.at[t, gather_b], s_gbz, r_gz.at[2], zdev).start()

    def gather_b_next():
        for d in range(2):
            blk = cgat.at[z * 4 + yprev[d], gather_b]
            remote(blk, blk, s_gbz, r_gz.at[3 + d], zdev).start()

    def gather_b_far():
        for d in range(2):
            drain(cgat.at[z * 4 + yfar, b_half(d)], r_ag.at[d, 5])
        blk = cgat.at[z * 4 + yfar, gather_b]
        remote(blk, blk, s_gbz, r_gz.at[5], zdev).start()

    loads[1].wait()
    gather_b_own()
    gather_own_z(0)

    for c in (loads[0], loads[2], loads[3]):
        c.wait()
    low_p = mm(acts[:, 0:128], olda[0], NT)
    for h in range(1, 4):
        low_p += mm(acts[:, h * 128 : (h + 1) * 128], olda[h], NT)
    thr_p = mm(cot[...], oldb[...], NT)
    part[...] = jnp.concatenate([low_p, thr_p], axis=1).astype(bf16).reshape(8, 32, 128)
    def send_part(k, _):
        remote(part.at[(t + k) % 8], prs.at[7 - k], s_prs, r_prs, tpeer(k)).start()
        return 0

    lax.fori_loop(1, 8, send_part, 0)

    gather_own_y(0)
    gather_b_twin()

    prow, pcol = iota((512, 512), 0), iota((512, 512), 1)
    blk = prow >> 4
    perma[...] = onehot(
        pcol == (((prow >> 2) & 3) << 7) + (((blk & 15) * 2 + (blk >> 4)) << 2) + (prow & 3)
    )
    erow, ecol = iota((512, 320), 0), iota((512, 320), 1)
    blk = erow >> 4
    idx = erow & 15
    spread[...] = onehot(
        (idx < 10) & (ecol == ((idx >> 1) << 6) + ((blk & 15) * 2 + (blk >> 4)) * 2 + (idx & 1))
    )
    erow, ecol = iota((320, 512), 1), iota((320, 512), 0)
    blk = erow >> 4
    idx = erow & 15
    gather[...] = onehot(
        (idx < 10) & (ecol == ((idx >> 1) << 6) + ((blk & 15) * 2 + (blk >> 4)) * 2 + (idx & 1))
    )
    rj, rk = iota((192, 192), 0), iota((192, 192), 1)
    permr[...] = onehot((rj - 3 * (rk & 63)) == (rk >> 6))
    slot = iota((16, 768), 1) - 48 * iota((16, 768), 0)
    slotm[...] = jnp.where((slot >= 0) & (slot < 48), slot, 1000)
    fr, fc = iota((192, 48), 0), iota((192, 48), 1)
    freshb[...] = jnp.where(((fr & 15) == (fc & 15)) & ((fc >> 4) <= (fr >> 6)), 0.0, -1e30).astype(f32)
    state[0].wait()
    diag = iota((128, 128), 0) == iota((128, 128), 1)
    lencol[...] = jnp.broadcast_to(
        jnp.sum(jnp.where(diag, len_ref[...].astype(f32), 0.0), axis=1, keepdims=True), (128, 128)
    )

    scale = f32(1.0) / jnp.sqrt(f32(128.0))

    def attend(g, _):
        rows = pl.ds(pl.multiple_of(g * 16, 16), 16)
        qg = jnp.concatenate(
            [q[s, rows, h * 128 : (h + 1) * 128] for s in range(3) for h in range(4)], axis=0
        )
        kg = keys[rows].reshape(768, 128)
        vg = vals[rows].reshape(768, 128)
        nkg = jnp.concatenate([nk[s, rows, :] for s in range(3)], axis=0)
        nvg = jnp.concatenate([nv[s, rows, :] for s in range(3)], axis=0)
        bias = jnp.where(slotm[...].astype(f32) < lencol[rows, 0:1], 0.0, -1e30).astype(f32)
        s1 = (mm(qg, kg, NT) * scale).reshape(12, 16, 768) + bias[None]
        s1 = s1.reshape(192, 768)
        s2 = mm(qg, nkg, NT) * scale + freshb[...]
        top = jnp.maximum(jnp.max(s1, axis=1, keepdims=True), jnp.max(s2, axis=1, keepdims=True))
        e1 = jnp.exp(s1 - top)
        e2 = jnp.exp(s2 - top)
        inv = 1.0 / (jnp.sum(e1, axis=1, keepdims=True) + jnp.sum(e2, axis=1, keepdims=True))
        o = mm((e1 * inv).astype(bf16), vg) + mm((e2 * inv).astype(bf16), nvg)
        o = o.astype(bf16)
        for s in range(3):
            for h in range(4):
                i = (s * 4 + h) * 16
                att[s, rows, h * 128 : (h + 1) * 128] = o[i : i + 16]
        return 0

    rows_a = pl.ds(0, 192)
    rows_b = pl.ds(192, 192)

    def order_rows(i):
        block = att[:, i * 64 : (i + 1) * 64, :].reshape(192, 512)
        attp[pl.ds(i * 192, 192)] = mm(permr[...], block).astype(bf16)

    def project(rows):
        def one(j, _):
            yb[j, rows] = mm(attp[rows], w[j]).astype(bf16)
            return 0

        return one

    this, other = z * 4, (1 - z) * 4

    def send_za(j, h):
        part_h = pl.ds(h * 96, 96)
        remote(yb.at[other + j, part_h], za.at[j, part_h], s_za, r_za.at[j], zdev).start()

    half_rows = 96
    classes = ((0, z), (192, z), (192, 1 - z))

    def part_of(c, owner, h):
        r0, plane = classes[c]
        return yb.at[plane * 4 + owner, pl.ds(r0 + h * half_rows, half_rows)]

    def y_far(c):
        for d in range(2):
            remote(part_of(c, yfar, d), far.at[c, d], s_p1.at[c], r_p1.at[c, d], ydev[d]).start()

    def y_raw(c):
        for d in range(2):
            remote(
                part_of(c, ynext[d], 1 - d), fin.at[c, d, 1 - d], s_raw.at[c], r_raw.at[c, d], ydev[d]
            ).start()

    def y_relay(c):
        for d in range(2):
            drain(far.at[c, d], r_p1.at[c, d])
            blk = part_of(c, ynext[d], d)
            blk[...] = (blk[...].astype(f32) + far[c, d].astype(f32)).astype(bf16)
            remote(blk, fin.at[c, d, d], s_p2.at[c], r_p2.at[c, d], ydev[d]).start()

    def y_total(c, h):
        return fin[c, 0, h].astype(f32) + fin[c, 1, h].astype(f32)

    def y_wait(c):
        for d in range(2):
            drain(fin.at[c, d, 1 - d], r_raw.at[c, d])
            drain(fin.at[c, d, d], r_p2.at[c, d])

    for c in loads[4:9]:
        c.wait()
    lax.fori_loop(0, 4, attend, 0)
    order_rows(0)

    gather_own_z(1)
    gather_own_y(1)
    drain(prs, r_prs)
    tot = part[t].astype(f32)
    for k in range(7):
        tot += prs[k].astype(f32)
    lows[...] = tot.astype(bf16)
    lowf[t] = tot.astype(bf16)

    def send_low(k, _):
        remote(lows, lowf.at[t], s_pag, r_pag, tpeer(k)).start()
        return 0

    lax.fori_loop(1, 8, send_low, 0)
    for c in loads[9:]:
        c.wait()
    lax.fori_loop(other, other + 4, project(rows_a), 0)
    gather_b_relay()
    gather_twin(0)
    send_za(yfar, 0)
    send_za(yfar, 1)
    lax.fori_loop(4, 6, attend, 0)

    gather_twin(1)
    gather_relay(0)
    drain(lowf.at[pl.ds(0, 7)], r_pag)

    both = lowf[...].reshape(256, 128)
    both_t = both.astype(f32).T.astype(bf16)
    ga_t = mm(both_t[64:128], acts[...]).astype(bf16)
    gb = mm(both_t[0:64], cot[...]).astype(bf16)
    ga = mm(perma[...], ga_t, NT)
    gb = jnp.concatenate([gb[:, c * 128 : (c + 1) * 128] for c in range(5)], axis=0)
    gb = mm(spread[...], gb)
    gst[:, 0:16, :] = gb.astype(bf16).reshape(32, 16, 128)
    gst[:, 16:32, :] = jnp.concatenate([ga, jnp.zeros_like(ga)], axis=1).astype(bf16).reshape(32, 16, 128)
    cc = remote(gst.at[pl.ds((1 - core) * 16, 16)], gpeer, s_core, r_core, corepeer)
    cc.start()
    send_za(ynext[0], 0)

    lax.fori_loop(6, 8, attend, 0)
    cc.wait_recv()
    hsum[...] = (gst[pl.ds(core * 16, 16)].astype(f32) + gpeer[...].astype(f32)).astype(bf16)

    for k in range(1, 4):
        remote(hsum.at[pl.ds((cx + k) % 4 * 4, 4)], xrecv.at[3 - k], s_dx, r_dx, xpeer(k)).start()
    send_za(ynext[0], 1)
    order_rows(1)
    lax.fori_loop(other, other + 4, project(rows_b), 0)
    y_far(2)
    lax.fori_loop(this, this + 4, project(rows_b), 0)
    y_far(1)
    drain(xrecv, r_dx)
    xtot = hsum[pl.ds(cx * 4, 4)].astype(f32)
    for k in range(3):
        xtot += xrecv[k].astype(f32)
    xsum[...] = xtot.astype(bf16)
    for k in range(1, 4):
        remote(xsum.at[(cz + k) % 4], zrecv.at[3 - k], s_dz, r_dz, zpeer(k)).start()
    send_za(ynext[1], 0)
    lax.fori_loop(this, this + 4, project(rows_a), 0)
    yown[...] = mm(attp[...], w[t])
    att2[...] = mm(attp[...], perma[...], NT).astype(bf16)
    def add_za(j):
        drain(za.at[j], r_za.at[j])
        blk = yb.at[this + j, rows_a]
        blk[...] = (blk[...].astype(f32) + za[j].astype(f32)).astype(bf16)

    gather_relay(1)
    add_za(yfar)
    y_far(0)
    y_raw(2)
    y_raw(1)

    drain(zrecv, r_dz)

    share = xsum[cz].astype(f32)
    for k in range(3):
        share += zrecv[k].astype(f32)
    share = share * (adapter_scale / 8192.0)
    for c in state[1:]:
        c.wait()
    gb_s[...] = share[0:16]
    ga_s[...] = share[16:32]
    for h in range(4):
        r = slice(h * 4, h * 4 + 4)
        new_p, new_m, new_v = adam_step(ma[h], oa[h], va[h], ga_s[r, 0:64])
        nma_o[h], noa_o[h], nva_o[h] = new_p, new_m, new_v
        ga_s[r, 0:64] = new_p
    for c in range(5):
        r = slice(c * 2, c * 2 + 2)
        l = slice(c * 128, (c + 1) * 128)
        new_p, new_m, new_v = adam_step(mb[:, l], ob[:, l], vb[:, l], gb_s[r, :])
        nmb_o[:, l], nob_o[:, l], nvb_o[:, l] = new_p, new_m, new_v
        gb_s[r, :] = new_p
    mine = core * 16 + chip
    fac[mine] = jnp.concatenate([gb_s[...], ga_s[...]], axis=0).astype(bf16)

    for k in range(1, 4):
        remote(fac.at[mine], fac.at[mine], s_fz, r_fz, zpeer(k)).start()
    send_za(ynext[1], 1)
    gather_b_next()
    gather_b_far()
    send_za(y, 0)

    thr = both[:, 64:128]
    add = [mm(thr, olda[h]) for h in range(4)]
    gacc[...] = adapter_scale * jnp.concatenate(add, axis=1) + mm(cot[...], w[t], NT)

    y_relay(2)
    y_relay(1)
    mycol = pl.ds(core * 16 + cx * 4, 4)
    drain(fac.at[pl.ds(0, 3)], r_fz)
    for k in range(1, 4):
        remote(fac.at[mycol], fac.at[mycol], s_fx, r_fx, xpeer(k)).start()

    for d in range(2):
        add_za(ynext[d])
    y_relay(0)
    y_raw(0)

    mycore = pl.ds(core * 16, 16)
    drain(fac.at[pl.ds(0, 12)], r_fx)
    fc = remote(fac.at[mycore], fac.at[mycore], s_fcore, r_fcore, corepeer)
    fc.start()
    fc.wait_recv()

    a_new = fac[:, 16:32, :].reshape(512, 128)
    low = mm(att2[...], a_new)[:, 0:64]
    low = jnp.concatenate([low[0:192], low[192:384]], axis=1)
    lsend[0] = low.astype(bf16)
    lz = remote(lsend.at[0], lpeer, s_lz, r_lz, zdev)
    lz.start()
    send_za(y, 1)
    b_new = mm(gather[...], fac[:, 0:16, :].reshape(512, 128)).astype(bf16)
    b_new = jnp.concatenate([b_new[c * 64 : (c + 1) * 64] for c in range(5)], axis=1)

    lz.wait_recv()
    low += lpeer[...].astype(f32)
    lsend[1] = low.astype(bf16)
    for k in range(1, 4):
        remote(lsend.at[1], lrecv.at[3 - k], s_low, r_low, (dp, this + (y + k) % 4)).start()

    y_wait(2)
    for h in range(2):
        blk = part_of(2, y, h)
        blk[...] = (blk[...].astype(f32) + y_total(2, h)).astype(bf16)
    zb = remote(yb.at[twin, rows_b], zbr, s_zb, r_zb, zdev)
    zb.start()

    for d in range(2):
        for p in range(2):
            drain(cgat.at[(other if p else this) + yprev[d], a_half(1 - d)], r_ag.at[d, 1 + p * 2 + 1 - d])
            drain(cgat.at[(other if p else this) + yfar, a_half(d)], r_ag.at[d, 6 + p])
        drain(cgat.at[other + yprev[d], gather_b], r_gz.at[3 + d])
    drain(cgat.at[twin, gather_b], r_gz.at[2])
    drain(cgat.at[other + yfar, gather_b], r_gz.at[5])

    def accumulate(k, _):
        src = jnp.where(k < 3, z, 1 - z) * 4 + (y + 1 + k) % 4
        gacc[...] += mm(cgat[src], w[src], NT)
        return 0

    lax.fori_loop(0, 7, accumulate, 0)
    grad_o[...] = gacc[...].astype(bf16)

    drain(lrecv, r_low)
    for k in range(3):
        low += lrecv[k].astype(f32)
    low = jnp.concatenate([low[:, 0:64], low[:, 64:128]], axis=0)
    hi = low.astype(bf16)
    lo = (low - hi.astype(f32)).astype(bf16)
    yown[...] += adapter_scale * (mm(hi, b_new) + mm(lo, b_new))

    drain(za.at[y], r_za.at[y])
    yown[rows_a] += za[y].astype(f32)
    y_wait(1)
    for h in range(2):
        yown[pl.ds(192 + h * half_rows, half_rows)] += y_total(1, h)
    zb.wait_recv()
    yown[rows_b] += zbr[...].astype(f32)
    y_wait(0)
    for h in range(2):
        yown[pl.ds(h * half_rows, half_rows)] += y_total(0, h)
    out_o[...] = yown[...].T.astype(bf16)

    cc.wait_send()
    fc.wait_send()
    zb.wait_send()
    lz.wait_send()
    drain(prs, s_prs)
    drain(lowf.at[pl.ds(0, 7)], s_pag)
    drain(cgat.at[0, pl.ds(96, 160)], s_gz)
    drain(cgat.at[pl.ds(0, 6), pl.ds(96, 160)], s_ag)
    drain(cgat.at[pl.ds(0, 3), gather_b], s_gb)
    drain(cgat.at[pl.ds(0, 4), gather_b], s_gbz)
    drain(xrecv, s_dx)
    drain(zrecv, s_dz)
    drain(fac.at[pl.ds(0, 3)], s_fz)
    drain(fac.at[pl.ds(0, 12)], s_fx)
    drain(za, s_za)
    for c in range(3):
        for sem in (s_p1, s_raw, s_p2):
            drain(far.at[c], sem.at[c])
    drain(lrecv, s_low)


def hand_over(*refs):
    n = (len(refs) - 1) // 2
    copies = [pltpu.make_async_copy(refs[i], refs[n + i], refs[-1].at[i]) for i in range(n)]
    for c in copies:
        c.start()
    for c in copies:
        c.wait()


def per_device(
    acts, cotangent, out_weight, old_a, old_b, master_a, master_b, moment_a, moment_b, second_a, second_b,
    key_cache, value_cache, lengths, new_query, new_key, new_value,
):
    hbm = pl.BlockSpec(memory_space=pl.ANY)
    vmem = pl.BlockSpec(memory_space=pltpu.VMEM)
    dma = pltpu.SemaphoreType.DMA
    V = pltpu.VMEM
    shp = jax.ShapeDtypeStruct
    results = pl.pallas_call(
        kernel,
        out_shape=(
            V((256, 512), bf16), V((4, 4, 64), f32), V((2, 640), f32), V((4, 4, 64), f32),
            V((2, 640), f32), V((4, 4, 64), f32), V((2, 640), f32), V((640, 384), bf16),
        ),
        in_specs=[hbm] * 17,
        out_specs=(vmem,) * 8,
        scratch_shapes=[
            V((256, 512), bf16), V((256, 640), bf16), V((8, 512, 640), bf16), V((4, 64, 128), bf16),
            V((64, 640), bf16), V((128, 48, 128), bf16), V((128, 48, 128), bf16), V((3, 128, 512), bf16),
            V((3, 128, 128), bf16), V((3, 128, 128), bf16),
            V((4, 4, 64), f32), V((2, 640), f32), V((4, 4, 64), f32), V((2, 640), f32),
            V((4, 4, 64), f32), V((2, 640), f32), V((1, 128), jnp.int32),
            V((512, 512), bf16), V((512, 320), bf16), V((320, 512), bf16), V((192, 192), bf16),
            V((16, 768), jnp.int32), V((192, 48), f32), V((128, 128), f32),
            V((8, 32, 128), bf16), V((7, 32, 128), bf16), V((32, 128), bf16), V((8, 32, 128), bf16),
            V((8, 256, 640), bf16), V((256, 512), f32),
            V((32, 32, 128), bf16), V((16, 32, 128), bf16), V((16, 32, 128), bf16), V((3, 4, 32, 128), bf16),
            V((4, 32, 128), bf16), V((3, 32, 128), bf16),
            V((16, 128), f32), V((16, 128), f32), V((32, 32, 128), bf16),
            V((3, 128, 512), bf16), V((384, 512), bf16), V((384, 512), bf16),
            V((8, 384, 640), bf16), V((384, 640), f32), V((4, 192, 640), bf16),
            V((3, 2, 96, 640), bf16), V((3, 2, 2, 96, 640), bf16), V((192, 640), bf16), V((2, 192, 128), bf16), V((192, 128), bf16),
            V((3, 192, 128), bf16),
            dma((24,)), dma, dma, dma, dma, dma, dma((2, 8)), dma, dma((6,)), dma, dma, dma, dma, dma, dma, dma, dma, dma, dma,
            dma, dma, dma, dma, dma, dma((4,)), dma((3,)), dma((3, 2)), dma((3,)), dma((3, 2)), dma((3,)), dma((3, 2)),
            dma, dma, dma, dma, dma, dma,
        ],
        compiler_params=pltpu.CompilerParams(
            collective_id=0, has_side_effects=True, vmem_limit_bytes=56 << 20
        ),
        cost_estimate=pl.CostEstimate(flops=4 << 30, bytes_accessed=12 << 20, transcendentals=1 << 20),
        name="update_and_decode",
    )(
        acts, cotangent, out_weight, old_a.swapaxes(1, 2), old_b,
        master_a, master_b, moment_a, moment_b, second_a, second_b,
        key_cache.reshape(128, 48, 128), value_cache.reshape(128, 48, 128), lengths.reshape(1, 128),
        new_query.swapaxes(0, 1), new_key.swapaxes(0, 1), new_value.swapaxes(0, 1),
    )
    return pl.pallas_call(
        hand_over,
        out_shape=tuple(shp(r.shape, r.dtype) for r in results),
        in_specs=[vmem] * 8,
        out_specs=(hbm,) * 8,
        scratch_shapes=[dma((8,))],
        cost_estimate=pl.CostEstimate(flops=0, bytes_accessed=2 << 20, transcendentals=0),
        name="hand_over",
    )(*(pltpu.with_memory_space_constraint(r, pltpu.VMEM) for r in results))


def solution(mesh):
    return jax.shard_map(
        per_device,
        mesh=mesh,
        in_specs=(
            P("dp", "tensor"),
            P("dp", "tensor"),
            P("tensor", None),
            P("tensor", None, None),
            P(),
            P("tensor", "dp", None),
            P("dp", "tensor"),
            P("tensor", "dp", None),
            P("dp", "tensor"),
            P("tensor", "dp", None),
            P("dp", "tensor"),
            P("dp", "tensor", None, None),
            P("dp", "tensor", None, None),
            P("dp"),
            P("dp", None, "tensor"),
            P("dp", None, "tensor"),
            P("dp", None, "tensor"),
        ),
        out_specs=(
            P("dp", "tensor"),
            P("tensor", "dp", None),
            P("dp", "tensor"),
            P("tensor", "dp", None),
            P("dp", "tensor"),
            P("tensor", "dp", None),
            P("dp", "tensor"),
            P("tensor", "dp"),
        ),
        check_vma=False,
    )
```

```python
import functools

import jax
import jax.numpy as jnp
from jax import lax
from jax.experimental import pallas as pl
from jax.experimental.pallas import tpu as pltpu
from jax.sharding import PartitionSpec as P

adapter_scale = 2.0
beta_one = 0.9
beta_two = 0.999
learn_rate = 0.01
decay_rate = 0.01
corr_one = 1.0 - 0.9**10
corr_two = 1.0 - 0.999**10
MESH = pl.DeviceIdType.MESH
f32 = jnp.float32
bf16 = jnp.bfloat16
NT = (((1,), (1,)), ((), ()))
NN = (((1,), (0,)), ((), ()))


def mm(a, b, dims=NN):
    return lax.dot_general(a, b, dims, preferred_element_type=f32)


def iota(shape, dim):
    return lax.broadcasted_iota(jnp.int32, shape, dim)


def onehot(hit):
    return jnp.where(hit, 1.0, 0.0).astype(f32).astype(bf16)


def adam_step(master, moment, second, grad):
    moment_new = beta_one * moment + (1.0 - beta_one) * grad
    second_new = beta_two * second + (1.0 - beta_two) * grad * grad
    update = moment_new / corr_one / (jnp.sqrt(second_new / corr_two) + 1e-08)
    return (master - learn_rate * (update + decay_rate * master), moment_new, second_new)


def kernel(
    acts_h, cot_h, w_h, olda_h, oldb_h,
    ma_h, mb_h, oa_h, ob_h, va_h, vb_h,
    key_h, val_h, len_h, q_h, nk_h, nv_h,
    grad_o, nma_o, nmb_o, noa_o, nob_o, nva_o, nvb_o, out_o,
    acts, cot, w, olda, oldb, keys, vals, q, nk, nv,
    ma, mb, oa, ob, va, vb, len_ref,
    perma, spread, gather, permr, slotm, freshb, lencol,
    part, prs, lows, lowf, cgat, gacc,
    gst, gpeer, hsum, xrecv, xsum, zrecv, ga_s, gb_s, fac,
    att, attp, att2, yb, yown, za, far, fin, zbr, lsend, lpeer, lrecv,
    lsem, s_prs, r_prs, s_pag, r_pag, s_ag, r_ag, s_gz, r_gz, s_gb, s_gbz, s_core, r_core, s_dx, r_dx, s_dz, r_dz,
    s_fz, r_fz, s_fx, r_fx, s_fcore, r_fcore, s_za, r_za, s_p1, r_p1, s_raw, r_raw, s_p2, r_p2, s_zb, r_zb, s_lz, r_lz, s_low, r_low,
):
    dp = lax.axis_index("dp")
    t = lax.axis_index("tensor")
    chip = dp // 2
    core = dp % 2
    z = t // 4
    y = t % 4

    def tpeer(k):
        return (dp, (t + k) % 8)

    cx, cz = chip // 4, chip % 4

    def xpeer(k):
        return ((((cx + k) % 4) * 4 + cz) * 2 + core, t)

    def zpeer(k):
        return ((cx * 4 + (cz + k) % 4) * 2 + core, t)

    corepeer = (chip * 2 + 1 - core, t)
    twin = (1 - z) * 4 + y
    zdev = (dp, twin)
    ynext = ((y + 1) % 4, (y + 3) % 4)
    yfar = (y + 2) % 4
    ydev = tuple((dp, z * 4 + n) for n in ynext)
    yprev = (ynext[1], ynext[0])

    def remote(src, dst, ssem, rsem, dev):
        return pltpu.make_async_remote_copy(
            src_ref=src, dst_ref=dst, send_sem=ssem, recv_sem=rsem, device_id=dev, device_id_type=MESH
        )

    def drain(ref, sem):
        pltpu.make_async_copy(ref, ref, sem).wait()

    loads = [
        pltpu.make_async_copy(acts_h, acts, lsem.at[0]),
        pltpu.make_async_copy(cot_h, cot, lsem.at[1]),
        pltpu.make_async_copy(olda_h, olda, lsem.at[2]),
        pltpu.make_async_copy(oldb_h.at[:, pl.ds(pl.multiple_of(t * 640, 128), 640)], oldb, lsem.at[3]),
        pltpu.make_async_copy(q_h, q, lsem.at[4]),
        pltpu.make_async_copy(key_h, keys, lsem.at[5]),
        pltpu.make_async_copy(nk_h, nk, lsem.at[6]),
        pltpu.make_async_copy(val_h, vals, lsem.at[7]),
        pltpu.make_async_copy(nv_h, nv, lsem.at[8]),
    ]
    for j in range(8):
        loads.append(pltpu.make_async_copy(w_h.at[:, pl.ds(j * 640, 640)], w.at[j], lsem.at[9 + j]))
    small = ((len_h, len_ref), (ma_h, ma), (mb_h, mb), (oa_h, oa), (ob_h, ob), (va_h, va), (vb_h, vb))
    state = [pltpu.make_async_copy(a, b, lsem.at[17 + i]) for i, (a, b) in enumerate(small)]
    for c in loads + state:
        c.start()

    bar = pltpu.get_barrier_semaphore()

    def sig_t(k, _):
        pl.semaphore_signal(bar, inc=1, device_id=tpeer(k), device_id_type=MESH)
        return 0

    def sig_c(k, _):
        pl.semaphore_signal(bar, inc=1, device_id=xpeer(k), device_id_type=MESH)
        pl.semaphore_signal(bar, inc=1, device_id=zpeer(k), device_id_type=MESH)
        return 0

    lax.fori_loop(1, 8, sig_t, 0)
    lax.fori_loop(1, 4, sig_c, 0)
    pl.semaphore_signal(bar, inc=1, device_id=corepeer, device_id_type=MESH)

    pl.semaphore_wait(bar, 14)

    gather_b = pl.ds(0, 96)

    def b_half(h):
        return pl.ds(h * 48, 48)

    def a_half(h):
        return pl.ds(96 + h * 80, 80)

    def gather_own_z(h):
        remote(cot.at[a_half(h)], cgat.at[t, a_half(h)], s_gz, r_gz.at[h], zdev).start()

    def gather_own_y(h):
        for d in range(2):
            remote(cot.at[a_half(h)], cgat.at[t, a_half(h)], s_ag, r_ag.at[d, 1 + h], ydev[d]).start()

    def gather_twin(h):
        blk = cgat.at[twin, a_half(h)]
        drain(blk, r_gz.at[h])
        for d in range(2):
            remote(blk, blk, s_ag, r_ag.at[d, 3 + h], ydev[d]).start()

    def gather_relay(which):
        for d in range(2):
            blk = cgat.at[(z if which == 0 else 1 - z) * 4 + yprev[d], a_half(d)]
            drain(blk, r_ag.at[d, 1 + which * 2 + d])
            remote(blk, blk, s_ag, r_ag.at[d, 6 + which], ydev[d]).start()

    def gather_b_own():
        for d in range(2):
            remote(cot.at[gather_b], cgat.at[t, gather_b], s_gb, r_ag.at[d, 0], ydev[d]).start()

    def gather_b_relay():
        for d in range(2):
            drain(cgat.at[z * 4 + yprev[d], gather_b], r_ag.at[d, 0])
            blk = cgat.at[z * 4 + yprev[d], b_half(d)]
            remote(blk, blk, s_gb, r_ag.at[d, 5], ydev[d]).start()

    def gather_b_twin():
        remote(cot.at[gather_b], cgat.at[t, gather_b], s_gbz, r_gz.at[2], zdev).start()

    def gather_b_next():
        for d in range(2):
            blk = cgat.at[z * 4 + yprev[d], gather_b]
            remote(blk, blk, s_gbz, r_gz.at[3 + d], zdev).start()

    def gather_b_far():
        for d in range(2):
            drain(cgat.at[z * 4 + yfar, b_half(d)], r_ag.at[d, 5])
        blk = cgat.at[z * 4 + yfar, gather_b]
        remote(blk, blk, s_gbz, r_gz.at[5], zdev).start()

    loads[1].wait()
    gather_b_own()
    gather_own_z(0)

    for c in (loads[0], loads[2], loads[3]):
        c.wait()
    low_p = mm(acts[:, 0:128], olda[0], NT)
    for h in range(1, 4):
        low_p += mm(acts[:, h * 128 : (h + 1) * 128], olda[h], NT)
    thr_p = mm(cot[...], oldb[...], NT)
    part[...] = jnp.concatenate([low_p, thr_p], axis=1).astype(bf16).reshape(8, 32, 128)
    def send_part(k, _):
        remote(part.at[(t + k) % 8], prs.at[7 - k], s_prs, r_prs, tpeer(k)).start()
        return 0

    lax.fori_loop(1, 8, send_part, 0)

    gather_own_y(0)
    gather_b_twin()

    prow, pcol = iota((512, 512), 0), iota((512, 512), 1)
    blk = prow >> 4
    perma[...] = onehot(
        pcol == (((prow >> 2) & 3) << 7) + (((blk & 15) * 2 + (blk >> 4)) << 2) + (prow & 3)
    )
    erow, ecol = iota((512, 320), 0), iota((512, 320), 1)
    blk = erow >> 4
    idx = erow & 15
    spread[...] = onehot(
        (idx < 10) & (ecol == ((idx >> 1) << 6) + ((blk & 15) * 2 + (blk >> 4)) * 2 + (idx & 1))
    )
    erow, ecol = iota((320, 512), 1), iota((320, 512), 0)
    blk = erow >> 4
    idx = erow & 15
    gather[...] = onehot(
        (idx < 10) & (ecol == ((idx >> 1) << 6) + ((blk & 15) * 2 + (blk >> 4)) * 2 + (idx & 1))
    )
    rj, rk = iota((192, 192), 0), iota((192, 192), 1)
    permr[...] = onehot((rj - 3 * (rk & 63)) == (rk >> 6))
    slot = iota((16, 768), 1) - 48 * iota((16, 768), 0)
    slotm[...] = jnp.where((slot >= 0) & (slot < 48), slot, 1000)
    fr, fc = iota((192, 48), 0), iota((192, 48), 1)
    freshb[...] = jnp.where(((fr & 15) == (fc & 15)) & ((fc >> 4) <= (fr >> 6)), 0.0, -1e30).astype(f32)
    state[0].wait()
    diag = iota((128, 128), 0) == iota((128, 128), 1)
    lencol[...] = jnp.broadcast_to(
        jnp.sum(jnp.where(diag, len_ref[...].astype(f32), 0.0), axis=1, keepdims=True), (128, 128)
    )

    scale = f32(1.0) / jnp.sqrt(f32(128.0))

    def attend(g, _):
        rows = pl.ds(pl.multiple_of(g * 16, 16), 16)
        qg = jnp.concatenate(
            [q[s, rows, h * 128 : (h + 1) * 128] for s in range(3) for h in range(4)], axis=0
        )
        kg = keys[rows].reshape(768, 128)
        vg = vals[rows].reshape(768, 128)
        nkg = jnp.concatenate([nk[s, rows, :] for s in range(3)], axis=0)
        nvg = jnp.concatenate([nv[s, rows, :] for s in range(3)], axis=0)
        bias = jnp.where(slotm[...].astype(f32) < lencol[rows, 0:1], 0.0, -1e30).astype(f32)
        s1 = (mm(qg, kg, NT) * scale).reshape(12, 16, 768) + bias[None]
        s1 = s1.reshape(192, 768)
        s2 = mm(qg, nkg, NT) * scale + freshb[...]
        top = jnp.maximum(jnp.max(s1, axis=1, keepdims=True), jnp.max(s2, axis=1, keepdims=True))
        e1 = jnp.exp(s1 - top)
        e2 = jnp.exp(s2 - top)
        inv = 1.0 / (jnp.sum(e1, axis=1, keepdims=True) + jnp.sum(e2, axis=1, keepdims=True))
        o = mm((e1 * inv).astype(bf16), vg) + mm((e2 * inv).astype(bf16), nvg)
        o = o.astype(bf16)
        for s in range(3):
            for h in range(4):
                i = (s * 4 + h) * 16
                att[s, rows, h * 128 : (h + 1) * 128] = o[i : i + 16]
        return 0

    rows_a = pl.ds(0, 192)
    rows_b = pl.ds(192, 192)

    def order_rows(i):
        block = att[:, i * 64 : (i + 1) * 64, :].reshape(192, 512)
        attp[pl.ds(i * 192, 192)] = mm(permr[...], block).astype(bf16)

    def project(rows):
        def one(j, _):
            yb[j, rows] = mm(attp[rows], w[j]).astype(bf16)
            return 0

        return one

    this, other = z * 4, (1 - z) * 4

    def send_za(j, h):
        part_h = pl.ds(h * 96, 96)
        remote(yb.at[other + j, part_h], za.at[j, part_h], s_za, r_za.at[j], zdev).start()

    half_rows = 96
    classes = ((0, z), (192, z), (192, 1 - z))

    def part_of(c, owner, h):
        r0, plane = classes[c]
        return yb.at[plane * 4 + owner, pl.ds(r0 + h * half_rows, half_rows)]

    def y_far(c):
        for d in range(2):
            remote(part_of(c, yfar, d), far.at[c, d], s_p1.at[c], r_p1.at[c, d], ydev[d]).start()

    def y_raw(c):
        for d in range(2):
            remote(
                part_of(c, ynext[d], 1 - d), fin.at[c, d, 1 - d], s_raw.at[c], r_raw.at[c, d], ydev[d]
            ).start()

    def y_relay(c):
        for d in range(2):
            drain(far.at[c, d], r_p1.at[c, d])
            blk = part_of(c, ynext[d], d)
            blk[...] = (blk[...].astype(f32) + far[c, d].astype(f32)).astype(bf16)
            remote(blk, fin.at[c, d, d], s_p2.at[c], r_p2.at[c, d], ydev[d]).start()

    def y_total(c, h):
        return fin[c, 0, h].astype(f32) + fin[c, 1, h].astype(f32)

    def y_wait(c):
        for d in range(2):
            drain(fin.at[c, d, 1 - d], r_raw.at[c, d])
            drain(fin.at[c, d, d], r_p2.at[c, d])

    for c in loads[4:9]:
        c.wait()
    lax.fori_loop(0, 4, attend, 0)
    order_rows(0)

    gather_own_z(1)
    gather_own_y(1)
    drain(prs, r_prs)
    tot = part[t].astype(f32)
    for k in range(7):
        tot += prs[k].astype(f32)
    lows[...] = tot.astype(bf16)
    lowf[t] = tot.astype(bf16)

    def send_low(k, _):
        remote(lows, lowf.at[t], s_pag, r_pag, tpeer(k)).start()
        return 0

    lax.fori_loop(1, 8, send_low, 0)
    for c in loads[9:]:
        c.wait()
    lax.fori_loop(other, other + 4, project(rows_a), 0)
    gather_b_relay()
    gather_twin(0)
    send_za(yfar, 0)
    send_za(yfar, 1)
    lax.fori_loop(4, 6, attend, 0)

    gather_twin(1)
    gather_relay(0)
    drain(lowf.at[pl.ds(0, 7)], r_pag)

    both = lowf[...].reshape(256, 128)
    both_t = both.astype(f32).T.astype(bf16)
    ga_t = mm(both_t[64:128], acts[...]).astype(bf16)
    gb = mm(both_t[0:64], cot[...]).astype(bf16)
    ga = mm(perma[...], ga_t, NT)
    gb = jnp.concatenate([gb[:, c * 128 : (c + 1) * 128] for c in range(5)], axis=0)
    gb = mm(spread[...], gb)
    gst[:, 0:16, :] = gb.astype(bf16).reshape(32, 16, 128)
    gst[:, 16:32, :] = jnp.concatenate([ga, jnp.zeros_like(ga)], axis=1).astype(bf16).reshape(32, 16, 128)
    cc = remote(gst.at[pl.ds((1 - core) * 16, 16)], gpeer, s_core, r_core, corepeer)
    cc.start()
    send_za(ynext[0], 0)

    lax.fori_loop(6, 8, attend, 0)
    cc.wait_recv()
    hsum[...] = (gst[pl.ds(core * 16, 16)].astype(f32) + gpeer[...].astype(f32)).astype(bf16)

    for k in range(1, 4):
        remote(hsum.at[pl.ds((cx + k) % 4 * 4, 4)], xrecv.at[3 - k], s_dx, r_dx, xpeer(k)).start()
    send_za(ynext[0], 1)
    order_rows(1)
    lax.fori_loop(other, other + 4, project(rows_b), 0)
    y_far(2)
    lax.fori_loop(this, this + 4, project(rows_b), 0)
    y_far(1)
    drain(xrecv, r_dx)
    xtot = hsum[pl.ds(cx * 4, 4)].astype(f32)
    for k in range(3):
        xtot += xrecv[k].astype(f32)
    xsum[...] = xtot.astype(bf16)
    for k in range(1, 4):
        remote(xsum.at[(cz + k) % 4], zrecv.at[3 - k], s_dz, r_dz, zpeer(k)).start()
    send_za(ynext[1], 0)
    lax.fori_loop(this, this + 4, project(rows_a), 0)
    yown[...] = mm(attp[...], w[t])
    att2[...] = mm(attp[...], perma[...], NT).astype(bf16)
    def add_za(j):
        drain(za.at[j], r_za.at[j])
        blk = yb.at[this + j, rows_a]
        blk[...] = (blk[...].astype(f32) + za[j].astype(f32)).astype(bf16)

    gather_relay(1)
    add_za(yfar)
    y_far(0)
    y_raw(2)
    y_raw(1)

    drain(zrecv, r_dz)

    share = xsum[cz].astype(f32)
    for k in range(3):
        share += zrecv[k].astype(f32)
    share = share * (adapter_scale / 8192.0)
    for c in state[1:]:
        c.wait()
    gb_s[...] = share[0:16]
    ga_s[...] = share[16:32]
    for h in range(4):
        r = slice(h * 4, h * 4 + 4)
        new_p, new_m, new_v = adam_step(ma[h], oa[h], va[h], ga_s[r, 0:64])
        nma_o[h], noa_o[h], nva_o[h] = new_p, new_m, new_v
        ga_s[r, 0:64] = new_p
    for c in range(5):
        r = slice(c * 2, c * 2 + 2)
        l = slice(c * 128, (c + 1) * 128)
        new_p, new_m, new_v = adam_step(mb[:, l], ob[:, l], vb[:, l], gb_s[r, :])
        nmb_o[:, l], nob_o[:, l], nvb_o[:, l] = new_p, new_m, new_v
        gb_s[r, :] = new_p
    mine = core * 16 + chip
    fac[mine] = jnp.concatenate([gb_s[...], ga_s[...]], axis=0).astype(bf16)

    for k in range(1, 4):
        remote(fac.at[mine], fac.at[mine], s_fz, r_fz, zpeer(k)).start()
    send_za(ynext[1], 1)
    gather_b_next()
    gather_b_far()

    thr = both[:, 64:128]
    add = [mm(thr, olda[h]) for h in range(4)]
    gacc[...] = adapter_scale * jnp.concatenate(add, axis=1) + mm(cot[...], w[t], NT)

    y_relay(2)
    y_relay(1)
    mycol = pl.ds(core * 16 + cx * 4, 4)
    drain(fac.at[pl.ds(0, 3)], r_fz)
    for k in range(1, 4):
        remote(fac.at[mycol], fac.at[mycol], s_fx, r_fx, xpeer(k)).start()

    for d in range(2):
        add_za(ynext[d])
    y_relay(0)

    mycore = pl.ds(core * 16, 16)
    drain(fac.at[pl.ds(0, 12)], r_fx)
    fc = remote(fac.at[mycore], fac.at[mycore], s_fcore, r_fcore, corepeer)
    fc.start()
    fc.wait_recv()

    a_new = fac[:, 16:32, :].reshape(512, 128)
    low = mm(att2[...], a_new)[:, 0:64]
    low = jnp.concatenate([low[0:192], low[192:384]], axis=1)
    lsend[0] = low.astype(bf16)
    lz = remote(lsend.at[0], lpeer, s_lz, r_lz, zdev)
    lz.start()
    send_za(y, 0)
    send_za(y, 1)
    b_new = mm(gather[...], fac[:, 0:16, :].reshape(512, 128)).astype(bf16)
    b_new = jnp.concatenate([b_new[c * 64 : (c + 1) * 64] for c in range(5)], axis=1)

    lz.wait_recv()
    low += lpeer[...].astype(f32)
    lsend[1] = low.astype(bf16)
    for k in range(1, 4):
        remote(lsend.at[1], lrecv.at[3 - k], s_low, r_low, (dp, this + (y + k) % 4)).start()
    y_raw(0)

    y_wait(2)
    for h in range(2):
        blk = part_of(2, y, h)
        blk[...] = (blk[...].astype(f32) + y_total(2, h)).astype(bf16)
    zb = remote(yb.at[twin, rows_b], zbr, s_zb, r_zb, zdev)
    zb.start()

    for d in range(2):
        for p in range(2):
            drain(cgat.at[(other if p else this) + yprev[d], a_half(1 - d)], r_ag.at[d, 1 + p * 2 + 1 - d])
            drain(cgat.at[(other if p else this) + yfar, a_half(d)], r_ag.at[d, 6 + p])
        drain(cgat.at[other + yprev[d], gather_b], r_gz.at[3 + d])
    drain(cgat.at[twin, gather_b], r_gz.at[2])
    drain(cgat.at[other + yfar, gather_b], r_gz.at[5])

    def accumulate(k, _):
        src = jnp.where(k < 3, z, 1 - z) * 4 + (y + 1 + k) % 4
        gacc[...] += mm(cgat[src], w[src], NT)
        return 0

    lax.fori_loop(0, 7, accumulate, 0)
    grad_o[...] = gacc[...].astype(bf16)

    drain(lrecv, r_low)
    for k in range(3):
        low += lrecv[k].astype(f32)
    low = jnp.concatenate([low[:, 0:64], low[:, 64:128]], axis=0)
    hi = low.astype(bf16)
    lo = (low - hi.astype(f32)).astype(bf16)
    yown[...] += adapter_scale * (mm(hi, b_new) + mm(lo, b_new))

    drain(za.at[y], r_za.at[y])
    yown[rows_a] += za[y].astype(f32)
    y_wait(1)
    for h in range(2):
        yown[pl.ds(192 + h * half_rows, half_rows)] += y_total(1, h)
    zb.wait_recv()
    yown[rows_b] += zbr[...].astype(f32)
    y_wait(0)
    for h in range(2):
        yown[pl.ds(h * half_rows, half_rows)] += y_total(0, h)
    out_o[...] = yown[...].T.astype(bf16)

    cc.wait_send()
    fc.wait_send()
    zb.wait_send()
    lz.wait_send()
    drain(prs, s_prs)
    drain(lowf.at[pl.ds(0, 7)], s_pag)
    drain(cgat.at[0, pl.ds(96, 160)], s_gz)
    drain(cgat.at[pl.ds(0, 6), pl.ds(96, 160)], s_ag)
    drain(cgat.at[pl.ds(0, 3), gather_b], s_gb)
    drain(cgat.at[pl.ds(0, 4), gather_b], s_gbz)
    drain(xrecv, s_dx)
    drain(zrecv, s_dz)
    drain(fac.at[pl.ds(0, 3)], s_fz)
    drain(fac.at[pl.ds(0, 12)], s_fx)
    drain(za, s_za)
    for c in range(3):
        for sem in (s_p1, s_raw, s_p2):
            drain(far.at[c], sem.at[c])
    drain(lrecv, s_low)


def hand_over(*refs):
    n = (len(refs) - 1) // 2
    copies = [pltpu.make_async_copy(refs[i], refs[n + i], refs[-1].at[i]) for i in range(n)]
    for c in copies:
        c.start()
    for c in copies:
        c.wait()


def per_device(
    acts, cotangent, out_weight, old_a, old_b, master_a, master_b, moment_a, moment_b, second_a, second_b,
    key_cache, value_cache, lengths, new_query, new_key, new_value,
):
    hbm = pl.BlockSpec(memory_space=pl.ANY)
    vmem = pl.BlockSpec(memory_space=pltpu.VMEM)
    dma = pltpu.SemaphoreType.DMA
    V = pltpu.VMEM
    shp = jax.ShapeDtypeStruct
    results = pl.pallas_call(
        kernel,
        out_shape=(
            V((256, 512), bf16), V((4, 4, 64), f32), V((2, 640), f32), V((4, 4, 64), f32),
            V((2, 640), f32), V((4, 4, 64), f32), V((2, 640), f32), V((640, 384), bf16),
        ),
        in_specs=[hbm] * 17,
        out_specs=(vmem,) * 8,
        scratch_shapes=[
            V((256, 512), bf16), V((256, 640), bf16), V((8, 512, 640), bf16), V((4, 64, 128), bf16),
            V((64, 640), bf16), V((128, 48, 128), bf16), V((128, 48, 128), bf16), V((3, 128, 512), bf16),
            V((3, 128, 128), bf16), V((3, 128, 128), bf16),
            V((4, 4, 64), f32), V((2, 640), f32), V((4, 4, 64), f32), V((2, 640), f32),
            V((4, 4, 64), f32), V((2, 640), f32), V((1, 128), jnp.int32),
            V((512, 512), bf16), V((512, 320), bf16), V((320, 512), bf16), V((192, 192), bf16),
            V((16, 768), jnp.int32), V((192, 48), f32), V((128, 128), f32),
            V((8, 32, 128), bf16), V((7, 32, 128), bf16), V((32, 128), bf16), V((8, 32, 128), bf16),
            V((8, 256, 640), bf16), V((256, 512), f32),
            V((32, 32, 128), bf16), V((16, 32, 128), bf16), V((16, 32, 128), bf16), V((3, 4, 32, 128), bf16),
            V((4, 32, 128), bf16), V((3, 32, 128), bf16),
            V((16, 128), f32), V((16, 128), f32), V((32, 32, 128), bf16),
            V((3, 128, 512), bf16), V((384, 512), bf16), V((384, 512), bf16),
            V((8, 384, 640), bf16), V((384, 640), f32), V((4, 192, 640), bf16),
            V((3, 2, 96, 640), bf16), V((3, 2, 2, 96, 640), bf16), V((192, 640), bf16), V((2, 192, 128), bf16), V((192, 128), bf16),
            V((3, 192, 128), bf16),
            dma((24,)), dma, dma, dma, dma, dma, dma((2, 8)), dma, dma((6,)), dma, dma, dma, dma, dma, dma, dma, dma, dma, dma,
            dma, dma, dma, dma, dma, dma((4,)), dma((3,)), dma((3, 2)), dma((3,)), dma((3, 2)), dma((3,)), dma((3, 2)),
            dma, dma, dma, dma, dma, dma,
        ],
        compiler_params=pltpu.CompilerParams(
            collective_id=0, has_side_effects=True, vmem_limit_bytes=56 << 20
        ),
        cost_estimate=pl.CostEstimate(flops=4 << 30, bytes_accessed=12 << 20, transcendentals=1 << 20),
        name="update_and_decode",
    )(
        acts, cotangent, out_weight, old_a.swapaxes(1, 2), old_b,
        master_a, master_b, moment_a, moment_b, second_a, second_b,
        key_cache.reshape(128, 48, 128), value_cache.reshape(128, 48, 128), lengths.reshape(1, 128),
        new_query.swapaxes(0, 1), new_key.swapaxes(0, 1), new_value.swapaxes(0, 1),
    )
    return pl.pallas_call(
        hand_over,
        out_shape=tuple(shp(r.shape, r.dtype) for r in results),
        in_specs=[vmem] * 8,
        out_specs=(hbm,) * 8,
        scratch_shapes=[dma((8,))],
        cost_estimate=pl.CostEstimate(flops=0, bytes_accessed=2 << 20, transcendentals=0),
        name="hand_over",
    )(*(pltpu.with_memory_space_constraint(r, pltpu.VMEM) for r in results))


def solution(mesh):
    return jax.shard_map(
        per_device,
        mesh=mesh,
        in_specs=(
            P("dp", "tensor"),
            P("dp", "tensor"),
            P("tensor", None),
            P("tensor", None, None),
            P(),
            P("tensor", "dp", None),
            P("dp", "tensor"),
            P("tensor", "dp", None),
            P("dp", "tensor"),
            P("tensor", "dp", None),
            P("dp", "tensor"),
            P("dp", "tensor", None, None),
            P("dp", "tensor", None, None),
            P("dp"),
            P("dp", None, "tensor"),
            P("dp", None, "tensor"),
            P("dp", None, "tensor"),
        ),
        out_specs=(
            P("dp", "tensor"),
            P("tensor", "dp", None),
            P("dp", "tensor"),
            P("tensor", "dp", None),
            P("dp", "tensor"),
            P("tensor", "dp", None),
            P("dp", "tensor"),
            P("tensor", "dp"),
        ),
        check_vma=False,
    )
```
